1024 devices in a mesh: replica: 32 (over x, y_hi, core), mp: 32 (over z, y_lo).
Axes of the slice: x: 4, y: 8 (y_hi: 4, y_lo: 2; y = y_hi * 2 + y_lo), z: 16, core: 2. Of those that a mesh axis runs over, the one named last changes fastest.
Arguments:
- table: float32 [32768, 256], P('mp'), may hold values from -0.6 to 0.6
- row_ids: int32 [32, 128], P('mp'), may hold values from 0 to 1023, as said below
- pool_counts: int32 [131072, 4096], P('replica', 'mp'), may hold values from 0 to 3
- table_of: int32 [32], replicated, may hold values from 0 to 7, as said below
- dense_feat: bfloat16 [13, 131072], P(None, ('replica', 'mp')), may hold values from -6 to 6
- labels: int32 [131072], P(('replica', 'mp')), may hold values 0 or 1
- w_bottom1: bfloat16 [13, 512], replicated, may hold values from -1.75 to 1.75
- w_bottom2: bfloat16 [512, 256], replicated, may hold values from -0.25 to 0.25
- cross_down: bfloat16 [2304, 256], replicated, may hold values from -0.125 to 0.125
- cross_up: bfloat16 [256, 2304], replicated, may hold values from -0.375 to 0.375
- w_top1: bfloat16 [2304, 512], replicated, may hold values from -0.125 to 0.125
- w_top2: bfloat16 [512, 512], replicated, may hold values from -0.25 to 0.25
- w_out: float32 [512], replicated, may hold values from -0.25 to 0.25
Outputs:
- row_grads: float32 [128, 8192], P('replica', 'mp')
- logits: float32 [131072], P(('replica', 'mp'))
The draws below stay inside these ranges and needn't reach their ends.
Inputs may be any that keep to these rules, and one draw needn't show every extreme that they name: `row_ids`: the 128 entries of each row are distinct. `table_of`: each table number appears exactly 4 times.
All inputs are finite; a program needn't handle non-finite values. No bound on the sum of `labels` on one device may be relied on, other than what follows from the above.
Results may differ from the reference program's by a relative error of at most 0.0084.
Values may be sent and summed in bfloat16 or wider, within the bound.
No kernel may reach another device: no remote copies, remote signals or barrier semaphores. Data moves between devices by JAX's collectives and lax.ppermute only.
A program may use at most 32 MiB of HBM per device.

```python
import jax
import jax.numpy as jnp
from jax import lax

E = 256
LR = 256
BOT = 512
TOP = 512
DENSE = 13
SHARDS = 4
LOOK = 128
ROWS_DEV = 1024
GROUPS = 32
NTAB = 8
D = 2304
B_GROUP = 4096
BATCH_ALL = 131072
TABLE_ROWS = 32768
N_MP = 32


def draw_row_ids(key, part):
    key = jax.random.fold_in(key, 11)
    device_keys = jax.random.split(key, N_MP)

    def one_shard(shard_key, shard):
        first_key, second_key = jax.random.split(shard_key)
        drawn = jax.random.permutation(first_key, ROWS_DEV)[:LOOK].astype(jnp.int32)
        others = jax.random.permutation(first_key, ROWS_DEV - 1)[:LOOK - 1].astype(jnp.int32)
        chosen = jnp.concatenate([jnp.full((1,), ROWS_DEV - 1, jnp.int32), others])
        placed = chosen[jax.random.permutation(second_key, LOOK)]
        return jnp.where(shard == 0, placed, drawn)
    return jax.vmap(one_shard)(device_keys, jnp.arange(N_MP, dtype=jnp.int32)).astype(jnp.int32)


def draw_pool_counts(key, part):
    key = jax.random.fold_in(key, 12)
    values = jax.random.randint(key, (BATCH_ALL, N_MP * LOOK), -12, 4)
    return jnp.maximum(values, 0).astype(jnp.int32)


def draw_table_of(key, part):
    key = jax.random.fold_in(key, 13)
    return (jax.random.permutation(key, N_MP) // SHARDS).astype(jnp.int32)


def touch_ends(result, stream_key, least, largest):
    longest = result.shape.index(max(result.shape))
    spots = []
    for shift in (0, 1):
        where = [jax.random.randint(jax.random.fold_in(stream_key, axis), (), 0, length) for axis, length in enumerate(result.shape)]
        where[longest] = (where[longest] + shift) % result.shape[longest]
        spots.append(tuple(where))
    return result.at[spots[0]].set(least).at[spots[1]].set(largest)


def steps_of(stream_key, dims, cuts, least, high):
    gain, own = 1.0, jax.random.fold_in(stream_key, 6)
    for axis_at, blocks in cuts:
        draws = jnp.exp(jax.random.uniform(jax.random.fold_in(own, axis_at), (blocks,), jnp.float32, least / len(cuts), high / len(cuts)))
        gain = gain * jnp.repeat(draws, dims[axis_at] // blocks).reshape([-1 if axis == axis_at else 1 for axis in range(len(dims))])
    return gain


def bell_draw(stream_key, dims, deviation, most, shards=(), held_as=jnp.bfloat16):
    factor_of = steps_of(stream_key, dims, shards, -0.22, 0.18) if shards else 1.0
    entries = jax.random.normal(stream_key, dims, jnp.float32) * deviation * factor_of
    return jnp.minimum(jnp.maximum(entries, -most), most).astype(held_as)


def setup_inputs(seed: int = 0) -> dict:
    seeds = jax.random.split(jax.random.key(seed), 14)
    table = bell_draw(seeds[0], (TABLE_ROWS, E), 0.1, 0.6, ((0, 32),), jnp.float32)
    row_ids = draw_row_ids(jax.random.fold_in(seeds[13], 71), 0)
    pool_counts = draw_pool_counts(jax.random.fold_in(seeds[13], 71), 0)
    table_of = draw_table_of(jax.random.fold_in(seeds[13], 71), 0)
    dense_feat = bell_draw(seeds[4], (DENSE, BATCH_ALL), 1.0, 6.0, ((1, 1024),))
    labels = touch_ends((jax.random.randint(seeds[5], (BATCH_ALL,), 0, 4) < 1).astype(jnp.int32), jax.random.fold_in(seeds[5], 1), 0, 1)
    w_bottom1 = bell_draw(seeds[6], (DENSE, BOT), DENSE ** -0.5, 1.75)
    w_bottom2 = bell_draw(seeds[7], (BOT, E), BOT ** -0.5, 0.25)
    cross_down = bell_draw(seeds[8], (D, LR), D ** -0.5, 0.125)
    cross_up = bell_draw(seeds[9], (LR, D), LR ** -0.5, 0.375)
    w_top1 = bell_draw(seeds[10], (D, TOP), D ** -0.5, 0.125)
    w_top2 = bell_draw(seeds[11], (TOP, TOP), TOP ** -0.5, 0.25)
    w_out = bell_draw(seeds[12], (TOP,), TOP ** -0.5, 0.25, (), jnp.float32)
    return {"table": table, "row_ids": row_ids, "pool_counts": pool_counts, "table_of": table_of, "dense_feat": dense_feat, "labels": labels, "w_bottom1": w_bottom1, "w_bottom2": w_bottom2, "cross_down": cross_down, "cross_up": cross_up, "w_top1": w_top1, "w_top2": w_top2, "w_out": w_out}


def silu_slope(value):
    sig = jax.nn.sigmoid(value)
    return sig + value * sig * (1.0 - sig)


def reference(table, row_ids, pool_counts, table_of, dense_feat, labels, w_bottom1, w_bottom2, cross_down, cross_up, w_top1, w_top2, w_out):
    shard_tables = table.reshape(N_MP, ROWS_DEV, E)
    looked = jax.vmap(lambda shard, index: jnp.take(shard, index, axis=0))(shard_tables, row_ids)
    onehot = (table_of[:, None] == jnp.arange(NTAB, dtype=jnp.int32)[None, :]).astype(jnp.float32)
    counts_all = pool_counts.reshape(GROUPS, B_GROUP, N_MP, LOOK)
    dense_all = dense_feat.reshape(DENSE, GROUPS, B_GROUP).transpose(1, 0, 2)
    labels_all = labels.reshape(GROUPS, B_GROUP)
    highest = lax.Precision.HIGHEST

    def per_group(running_sum, inputs):
        counts, dense_cols, clicks = inputs
        counts_f = counts.astype(jnp.float32)
        pooled = jnp.einsum("bmj,mje->bme", counts_f, looked, precision=highest).astype(jnp.bfloat16)
        pooled_emb = jnp.einsum("bme,mt->bte", pooled.astype(jnp.float32), onehot, precision=highest).astype(jnp.bfloat16)
        hidden = jax.nn.relu(jnp.dot(dense_cols.T, w_bottom1, preferred_element_type=jnp.float32)).astype(jnp.bfloat16)
        bottom = jax.nn.relu(jnp.dot(hidden, w_bottom2, preferred_element_type=jnp.float32)).astype(jnp.bfloat16)
        features = jnp.concatenate([bottom, pooled_emb.reshape(B_GROUP, NTAB * E)], axis=1)
        low_rank = jnp.dot(features, cross_down, preferred_element_type=jnp.float32).astype(jnp.bfloat16)
        cross_scale = jnp.dot(low_rank, cross_up, preferred_element_type=jnp.float32)
        feat_f = features.astype(jnp.float32)
        crossed = (feat_f * cross_scale + feat_f).astype(jnp.bfloat16)
        pre_one = jnp.dot(crossed, w_top1, preferred_element_type=jnp.float32)
        act_one = jax.nn.silu(pre_one).astype(jnp.bfloat16)
        pre_two = jnp.dot(act_one, w_top2, preferred_element_type=jnp.float32)
        logits = jnp.sum(jax.nn.silu(pre_two) * w_out[None, :], axis=1)
        logit_grad = (jax.nn.sigmoid(logits) - clicks.astype(jnp.float32)) / GROUPS
        grad_two = (logit_grad[:, None] * w_out[None, :] * silu_slope(pre_two)).astype(jnp.bfloat16)
        grad_act = jnp.dot(grad_two, w_top2.T, preferred_element_type=jnp.float32)
        grad_one = (grad_act * silu_slope(pre_one)).astype(jnp.bfloat16)
        crossed_grad = jnp.dot(grad_one, w_top1.T, preferred_element_type=jnp.float32)
        scale_grad = (crossed_grad * feat_f).astype(jnp.bfloat16)
        low_grad = jnp.dot(scale_grad, cross_up.T, preferred_element_type=jnp.float32).astype(jnp.bfloat16)
        feature_grad = crossed_grad * (cross_scale + 1.0) + jnp.dot(low_grad, cross_down.T, preferred_element_type=jnp.float32)
        emb_grad = feature_grad[:, E:].astype(jnp.bfloat16).reshape(B_GROUP, NTAB, E)
        pooled_grad = jnp.einsum("bte,mt->bme", emb_grad.astype(jnp.float32), onehot, precision=highest).astype(jnp.bfloat16)
        running_sum = running_sum + jnp.einsum("bmj,bme->mje", counts_f, pooled_grad.astype(jnp.float32), precision=highest)
        return running_sum, logits

    start_sum = jnp.zeros((N_MP, LOOK, E), jnp.float32)
    grads, logits = lax.scan(per_group, start_sum, (counts_all, dense_all, labels_all))
    row_grads = grads.transpose(1, 0, 2).reshape(LOOK, N_MP * E)
    return row_grads, logits.reshape(GROUPS * B_GROUP)
```

```python
import functools

import jax
import jax.numpy as jnp
from jax import lax
from jax.experimental import pallas as pl
from jax.experimental.pallas import tpu as pltpu
from jax.sharding import Mesh
from jax.sharding import PartitionSpec as P

X, YH, CORES, Z, YL = 4, 4, 2, 16, 2
REP = ("x", "yh", "c")
MP = ("z", "yl")
SHARDS = Z * YL
TABLES = 8
PER = SHARDS // TABLES
E = 256
N = 128
LOOK = 128
BF = jnp.bfloat16
F32 = jnp.float32


def silu_slope(value, sig):
    return sig + value * sig * (1.0 - sig)


def dot(a, b):
    return jnp.dot(a, b, preferred_element_type=F32)


def dot_nt(a, b):
    return lax.dot_general(a, b, (((1,), (1,)), ((), ())), preferred_element_type=F32)


def dot_tn(a, b):
    return lax.dot_general(a, b, (((0,), (0,)), ((), ())), preferred_element_type=F32)


def step_kernel(
    place,
    table_of,
    counts,
    looked,
    bottom,
    labels,
    cross_down,
    cross_up,
    w_top1,
    w_top2,
    w_out,
    grads,
    logits_out,
    feats,
    scaled,
    emb_grad,
    order,
    filled,
):
    my_x, my_c = place[0], place[1]
    for t in range(TABLES):
        filled[t] = 0
    for m in range(SHARDS):
        t = table_of[m]
        k = filled[t]
        order[t * PER + k] = m
        filled[t] = k + 1

    def cols(k):
        return slice(k * E, (k + 1) * E)

    feats[:, cols(0)] = bottom[...]
    for t in range(TABLES):
        acc = None
        for k in range(PER):
            m = order[t * PER + k]
            rows = jnp.concatenate(
                [
                    looked[lax.bitwise_xor(my_c, c), lax.rem(my_x + X - x, X), m]
                    for c in range(CORES)
                    for x in range(X)
                ],
                axis=0,
            )
            term = dot(counts[m], rows)
            acc = term if acc is None else acc + term
        feats[:, cols(t + 1)] = acc.astype(BF)

    low = dot(feats[...], cross_down[...]).astype(BF)
    pre_one = None
    for k in range(TABLES + 1):
        scale = dot(low, cross_up[:, cols(k)])
        scaled[:, cols(k)] = scale
        feat = feats[:, cols(k)].astype(F32)
        term = dot((feat * scale + feat).astype(BF), w_top1[cols(k), :])
        pre_one = term if pre_one is None else pre_one + term
    sig_one = jax.nn.sigmoid(pre_one)
    pre_two = dot((pre_one * sig_one).astype(BF), w_top2[...])
    sig_two = jax.nn.sigmoid(pre_two)
    head = w_out[...]
    logits = jnp.sum(pre_two * sig_two * head, axis=1, keepdims=True)
    logits_out[...] = logits
    logit_grad = (jax.nn.sigmoid(logits) - labels[...].astype(F32)) * (1.0 / 32.0)
    grad_two = (logit_grad * head * silu_slope(pre_two, sig_two)).astype(BF)
    grad_one = (dot_nt(grad_two, w_top2[...]) * silu_slope(pre_one, sig_one)).astype(BF)
    low_grad = None
    for k in range(TABLES + 1):
        part = dot_nt(grad_one, w_top1[cols(k), :])
        feat = feats[:, cols(k)].astype(F32)
        term = dot_nt((part * feat).astype(BF), cross_up[:, cols(k)])
        low_grad = term if low_grad is None else low_grad + term
        if k > 0:
            scaled[:, cols(k)] = part * (scaled[:, cols(k)] + 1.0)
    low_grad = low_grad.astype(BF)
    for t in range(TABLES):
        back = dot_nt(low_grad, cross_down[cols(t + 1), :])
        emb_grad[t] = (scaled[:, cols(t + 1)] + back).astype(BF)

    def one_shard(m, carry):
        terms = dot_tn(counts[m], emb_grad[table_of[m]]).astype(BF)
        for c in range(CORES):
            for x in range(X):
                at = (c * X + x) * 16
                grads[c, x, m] = terms[at : at + 16]
        return carry

    lax.fori_loop(0, SHARDS, one_shard, 0, unroll=4)


def run_step(place, table_of, *arrays):
    smem = pl.BlockSpec(memory_space=pltpu.SMEM)
    vmem = pl.BlockSpec(memory_space=pltpu.VMEM)
    return pl.pallas_call(
        step_kernel,
        out_shape=(
            jax.ShapeDtypeStruct((CORES, X, SHARDS, 16, E), BF),
            jax.ShapeDtypeStruct((N, 1), F32),
        ),
        in_specs=[smem, smem] + [vmem] * len(arrays),
        out_specs=(vmem, vmem),
        scratch_shapes=[
            pltpu.VMEM((N, (TABLES + 1) * E), BF),
            pltpu.VMEM((N, (TABLES + 1) * E), F32),
            pltpu.VMEM((TABLES, N, E), BF),
            pltpu.SMEM((SHARDS,), jnp.int32),
            pltpu.SMEM((TABLES,), jnp.int32),
        ],
        compiler_params=pltpu.CompilerParams(vmem_limit_bytes=40 * 2**20),
        cost_estimate=pl.CostEstimate(
            flops=3 * 10**9, bytes_accessed=12 * 2**20, transcendentals=2 * 10**5
        ),
    )(place, table_of, *arrays)


def swap(value, axes):
    return lax.all_to_all(value, axes, split_axis=0, concat_axis=0, tiled=True)


def add_up(value):
    return jnp.sum(value.astype(F32), axis=0)


def turn(value, axis, size, shift):
    return lax.ppermute(value, axis, [(i, (i + shift) % size) for i in range(size)])


def shards(
    table,
    row_ids,
    pool_counts,
    table_of,
    dense_feat,
    labels,
    w_bottom1,
    w_bottom2,
    cross_down,
    cross_up,
    w_top1,
    w_top2,
    w_out,
):
    my_x, my_c = lax.axis_index("x"), lax.axis_index("c")
    ids = row_ids[0].reshape(X, YH, CORES, 4).transpose(2, 0, 1, 3)
    ids = lax.dynamic_index_in_dim(ids.reshape(CORES * X, 16), my_c * X + my_x, 0, keepdims=False)
    mine = jnp.take(table, ids, axis=0).astype(BF)
    looked = swap(jnp.broadcast_to(mine, (SHARDS, 16, E)), MP)
    counts = pool_counts.astype(BF).reshape(SHARDS * N, X, YH, CORES, 4)
    counts = counts.transpose(0, 3, 1, 2, 4).reshape(SHARDS, N, LOOK)
    counts, looked = lax.optimization_barrier((counts, looked))
    counts = swap(counts, MP)
    looked = jnp.stack([looked] + [turn(looked, "x", X, k) for k in range(1, X)])
    looked = jnp.stack([looked, turn(looked, "c", CORES, 1)])

    hidden = lax.dot_general(
        dense_feat, w_bottom1, (((0,), (0,)), ((), ())), preferred_element_type=F32
    )
    hidden = jax.nn.relu(hidden).astype(BF)
    bottom = jax.nn.relu(dot(hidden, w_bottom2)).astype(BF)

    place = jnp.stack([my_x, my_c]).astype(jnp.int32)
    grads, logits = run_step(
        place,
        table_of,
        counts,
        looked,
        bottom,
        labels.reshape(N, 1),
        cross_down,
        cross_up,
        w_top1,
        w_top2,
        w_out.reshape(1, -1),
    )
    grads = add_up(swap(grads, "c")).astype(BF)
    grads = add_up(swap(grads, "x")).astype(BF)
    grads = grads.reshape(SHARDS, YH, 4, E).transpose(1, 0, 2, 3)
    grads = add_up(swap(grads, "yh")).astype(BF)
    grads = add_up(swap(grads, MP))
    return grads, logits.reshape(N)


def solution(mesh):
    fine = Mesh(mesh.devices.reshape(X, YH, CORES, Z, YL), REP + MP)
    both = REP + MP
    return jax.shard_map(
        shards,
        mesh=fine,
        in_specs=(
            P(MP, None),
            P(MP, None),
            P(REP, MP),
            P(),
            P(None, both),
            P(both),
            P(),
            P(),
            P(),
            P(),
            P(),
            P(),
            P(),
        ),
        out_specs=(P(REP, MP), P(both)),
        check_vma=False,
    )
```

```python
import functools

import jax
import jax.numpy as jnp
from jax import lax
from jax.experimental import pallas as pl
from jax.experimental.pallas import tpu as pltpu
from jax.sharding import Mesh
from jax.sharding import PartitionSpec as P

X, YH, CORES, Z, YL = 4, 4, 2, 16, 2
REP = ("x", "yh", "c")
MP = ("z", "yl")
SHARDS = Z * YL
TABLES = 8
PER = SHARDS // TABLES
E = 256
N = 128
LOOK = 128
BF = jnp.bfloat16
F32 = jnp.float32


def silu_slope(value, sig):
    return sig + value * sig * (1.0 - sig)


def dot(a, b):
    return jnp.dot(a, b, preferred_element_type=F32)


def dot_nt(a, b):
    return lax.dot_general(a, b, (((1,), (1,)), ((), ())), preferred_element_type=F32)


def dot_tn(a, b):
    return lax.dot_general(a, b, (((0,), (0,)), ((), ())), preferred_element_type=F32)


def split_dot(value, weights):
    high = value.astype(BF)
    low = (value - high.astype(F32)).astype(BF)
    return dot(high, weights) + dot(low, weights)


def cols(k):
    return slice(k * E, (k + 1) * E)


def step_kernel(
    place,
    table_of,
    counts,
    looked,
    bottom,
    labels,
    w_out,
    down_hbm,
    up_hbm,
    top1_hbm,
    top2_hbm,
    grads,
    logits_out,
    cross_down,
    cross_up,
    w_top1,
    w_top2,
    feats,
    scaled,
    emb_grad,
    order,
    filled,
    arrived,
):
    copies = [
        pltpu.make_async_copy(source, target, arrived.at[i])
        for i, (source, target) in enumerate(
            (
                (down_hbm, cross_down),
                (up_hbm, cross_up),
                (top1_hbm, w_top1),
                (top2_hbm, w_top2),
            )
        )
    ]
    for copy in copies:
        copy.start()
    my_x, my_c = place[0], place[1]
    for t in range(TABLES):
        filled[t] = 0
    for m in range(SHARDS):
        t = table_of[m]
        k = filled[t]
        order[t * PER + k] = m
        filled[t] = k + 1

    feats[:, cols(0)] = bottom[...].astype(F32)
    for t in range(TABLES):
        acc = None
        for k in range(PER):
            m = order[t * PER + k]
            rows = jnp.concatenate(
                [
                    looked[lax.bitwise_xor(my_c, c), lax.rem(my_x + X - x, X), m]
                    for x in range(X)
                    for c in range(CORES)
                ],
                axis=0,
            )
            term = dot(counts[m], rows)
            acc = term if acc is None else acc + term
        feats[:, cols(t + 1)] = acc

    copies[0].wait()
    low = split_dot(feats[...], cross_down[...])
    low_high = low.astype(BF)
    low_rest = (low - low_high.astype(F32)).astype(BF)
    copies[1].wait()
    copies[2].wait()
    pre_one = None
    for k in range(TABLES + 1):
        scale = dot(low_high, cross_up[:, cols(k)]) + dot(low_rest, cross_up[:, cols(k)])
        scaled[:, cols(k)] = scale
        feat = feats[:, cols(k)]
        term = split_dot(feat * scale + feat, w_top1[cols(k), :])
        pre_one = term if pre_one is None else pre_one + term
    copies[3].wait()
    sig_one = jax.nn.sigmoid(pre_one)
    pre_two = split_dot(pre_one * sig_one, w_top2[...])
    sig_two = jax.nn.sigmoid(pre_two)
    head = w_out[...]
    logits = jnp.sum(pre_two * sig_two * head, axis=1, keepdims=True)
    logits_out[...] = logits
    logit_grad = (jax.nn.sigmoid(logits) - labels[...].astype(F32)) * (1.0 / 32.0)
    grad_two = (logit_grad * head * silu_slope(pre_two, sig_two)).astype(BF)
    grad_one = (dot_nt(grad_two, w_top2[...]) * silu_slope(pre_one, sig_one)).astype(BF)
    low_grad = None
    for k in range(TABLES + 1):
        part = dot_nt(grad_one, w_top1[cols(k), :])
        term = dot_nt((part * feats[:, cols(k)]).astype(BF), cross_up[:, cols(k)])
        low_grad = term if low_grad is None else low_grad + term
        if k > 0:
            scaled[:, cols(k)] = part * (scaled[:, cols(k)] + 1.0)
    low_grad = low_grad.astype(BF)
    for t in range(TABLES):
        back = dot_nt(low_grad, cross_down[cols(t + 1), :])
        emb_grad[t] = (scaled[:, cols(t + 1)] + back).astype(BF)

    to = lax.broadcasted_iota(jnp.int32, (LOOK, LOOK), 0)
    at = lax.broadcasted_iota(jnp.int32, (LOOK, LOOK), 1)
    source = (to // 16 % X) * 32 + (to // 4 % YH) * 8 + (to // 64) * 4 + to % 4
    turned = (at == source).astype(BF)

    def one_shard(m, carry):
        picked = dot_nt(turned, counts[m]).astype(BF)
        terms = dot(picked, emb_grad[table_of[m]]).astype(BF)
        for c in range(CORES):
            for x in range(X):
                at = (c * X + x) * 16
                grads[c, x, m] = terms[at : at + 16]
        return carry

    lax.fori_loop(0, SHARDS, one_shard, 0, unroll=4)


def run_step(place, table_of, arrays, weights):
    smem = pl.BlockSpec(memory_space=pltpu.SMEM)
    vmem = pl.BlockSpec(memory_space=pltpu.VMEM)
    hbm = pl.BlockSpec(memory_space=pltpu.HBM)
    return pl.pallas_call(
        step_kernel,
        out_shape=(
            jax.ShapeDtypeStruct((CORES, X, SHARDS, 16, E), BF),
            jax.ShapeDtypeStruct((N, 1), F32),
        ),
        in_specs=[smem, smem] + [vmem] * len(arrays) + [hbm] * len(weights),
        out_specs=(vmem, vmem),
        scratch_shapes=[pltpu.VMEM(w.shape, w.dtype) for w in weights]
        + [
            pltpu.VMEM((N, (TABLES + 1) * E), F32),
            pltpu.VMEM((N, (TABLES + 1) * E), F32),
            pltpu.VMEM((TABLES, N, E), BF),
            pltpu.SMEM((SHARDS,), jnp.int32),
            pltpu.SMEM((TABLES,), jnp.int32),
            pltpu.SemaphoreType.DMA((len(weights),)),
        ],
        compiler_params=pltpu.CompilerParams(vmem_limit_bytes=32 * 2**20),
        cost_estimate=pl.CostEstimate(
            flops=4 * 10**9, bytes_accessed=12 * 2**20, transcendentals=2 * 10**5
        ),
    )(place, table_of, *arrays, *weights)


def pair_kernel(halves, out):
    to = lax.broadcasted_iota(jnp.int32, (E, E), 0)
    at = lax.broadcasted_iota(jnp.int32, (E, E), 1)
    turned = (at == (to // 4 % Z) * 16 + (to // 64) * 4 + to % 4).astype(BF)
    for x in range(X):
        for yl in range(YL):
            rows = jnp.concatenate(
                [
                    (
                        halves[0, x, z * YL + yl].astype(F32)
                        + halves[1, x, z * YL + yl].astype(F32)
                    ).astype(BF)
                    for z in range(Z)
                ],
                axis=0,
            )
            rows = dot(turned, rows).astype(BF)
            for yh in range(YH):
                out[x, yh, yl] = rows[yh * 64 : yh * 64 + 64]


def add_pair(halves):
    return pl.pallas_call(
        pair_kernel,
        out_shape=jax.ShapeDtypeStruct((X, YH, YL, Z * 4, E), BF),
        in_specs=[pl.BlockSpec(memory_space=pltpu.VMEM)],
        out_specs=pl.BlockSpec(memory_space=pltpu.VMEM),
        compiler_params=pltpu.CompilerParams(vmem_limit_bytes=16 * 2**20),
        cost_estimate=pl.CostEstimate(
            flops=3 * 10**8, bytes_accessed=3 * 2**20, transcendentals=0
        ),
    )(halves)


def swap(value, axes):
    return lax.all_to_all(value, axes, split_axis=0, concat_axis=0, tiled=True)


def add_up(value):
    return jnp.sum(value.astype(F32), axis=0)


def turn(value, axis, size, shift):
    return lax.ppermute(value, axis, [(i, (i + shift) % size) for i in range(size)])


def shards(
    table,
    row_ids,
    pool_counts,
    table_of,
    dense_feat,
    labels,
    w_bottom1,
    w_bottom2,
    cross_down,
    cross_up,
    w_top1,
    w_top2,
    w_out,
):
    my_x, my_c = lax.axis_index("x"), lax.axis_index("c")
    ids = lax.dynamic_slice(row_ids, (0, (my_x * CORES + my_c) * 16), (1, 16))[0]
    mine = jnp.take(table, ids, axis=0, mode="clip").astype(BF)
    mine = jnp.broadcast_to(mine, (SHARDS, 16, E))
    mine, pool_counts = lax.optimization_barrier((mine, pool_counts))
    looked = swap(mine, MP)
    counts = swap(pool_counts.astype(BF).reshape(SHARDS, N, LOOK), MP)
    looked = jnp.stack([looked] + [turn(looked, "x", X, k) for k in range(1, X)])
    looked = jnp.stack([looked, turn(looked, "c", CORES, 1)])

    hidden = lax.dot_general(
        dense_feat, w_bottom1, (((0,), (0,)), ((), ())), preferred_element_type=F32
    )
    hidden = jax.nn.relu(hidden).astype(BF)
    bottom = jax.nn.relu(dot(hidden, w_bottom2)).astype(BF)

    place = jnp.stack([my_x, my_c]).astype(jnp.int32)
    grads, logits = run_step(
        place,
        table_of,
        (counts, looked, bottom, labels.reshape(N, 1), w_out.reshape(1, -1)),
        (cross_down, cross_up, w_top1, w_top2),
    )
    grads = add_pair(swap(grads, "c")).reshape(X * YH * YL, Z * 4, E)
    grads = add_up(swap(grads, ("x", "yh", "yl"))).astype(BF)
    grads = add_up(swap(grads.reshape(Z, 4, E), "z"))
    return grads, logits.reshape(N)


def solution(mesh):
    fine = Mesh(mesh.devices.reshape(X, YH, CORES, Z, YL), REP + MP)
    both = REP + MP
    return jax.shard_map(
        shards,
        mesh=fine,
        in_specs=(
            P(MP, None),
            P(MP, None),
            P(REP, MP),
            P(),
            P(None, both),
            P(both),
            P(),
            P(),
            P(),
            P(),
            P(),
            P(),
            P(),
        ),
        out_specs=(P(REP, MP), P(both)),
        check_vma=False,
    )
```

```python
import functools

import jax
import jax.numpy as jnp
from jax import lax
from jax.experimental import pallas as pl
from jax.experimental.pallas import tpu as pltpu
from jax.sharding import Mesh
from jax.sharding import PartitionSpec as P

X, YH, CORES, Z, YL = 4, 4, 2, 16, 2
REP = ("x", "yh", "c")
MP = ("z", "yl")
SHARDS = Z * YL
TABLES = 8
PER = SHARDS // TABLES
E = 256
N = 128
LOOK = 128
BF = jnp.bfloat16
F32 = jnp.float32


def silu_slope(value, sig):
    return sig + value * sig * (1.0 - sig)


def dot(a, b):
    return jnp.dot(a, b, preferred_element_type=F32)


def dot_nt(a, b):
    return lax.dot_general(a, b, (((1,), (1,)), ((), ())), preferred_element_type=F32)


def dot_tn(a, b):
    return lax.dot_general(a, b, (((0,), (0,)), ((), ())), preferred_element_type=F32)


def split_dot(value, weights):
    high = value.astype(BF)
    low = (value - high.astype(F32)).astype(BF)
    return dot(high, weights) + dot(low, weights)


def cols(k):
    return slice(k * E, (k + 1) * E)


def step_kernel(
    place,
    table_of,
    bottom,
    labels,
    w_out,
    counts_hbm,
    own_hbm,
    other_hbm,
    down_hbm,
    up_hbm,
    top1_hbm,
    top2_hbm,
    grads,
    logits_out,
    counts,
    looked,
    cross_down,
    cross_up,
    w_top1,
    w_top2,
    feats,
    scaled,
    emb_grad,
    order,
    filled,
    arrived,
):
    moves = (
        (counts_hbm, counts),
        (own_hbm, looked.at[0]),
        (other_hbm, looked.at[1]),
        (down_hbm, cross_down),
        (up_hbm, cross_up),
        (top1_hbm, w_top1),
        (top2_hbm, w_top2),
    )
    copies = [pltpu.make_async_copy(*move, arrived.at[i]) for i, move in enumerate(moves)]
    for copy in copies:
        copy.start()
    my_x, my_yh, my_c = place[0], place[1], place[2]
    for t in range(TABLES):
        filled[t] = 0
    for m in range(SHARDS):
        t = table_of[m]
        k = filled[t]
        order[t * PER + k] = m
        filled[t] = k + 1

    feats[:, cols(0)] = bottom[...].astype(F32)
    for copy in copies[:3]:
        copy.wait()
    for t in range(TABLES):
        acc = None
        for k in range(PER):
            m = order[t * PER + k]
            rows = jnp.concatenate(
                [
                    looked[lax.bitwise_xor(my_c, c), lax.rem(my_x + X - x, X), m]
                    for c in range(CORES)
                    for x in range(X)
                ],
                axis=0,
            )
            term = dot(counts[m], rows)
            acc = term if acc is None else acc + term
        feats[:, cols(t + 1)] = acc

    copies[3].wait()
    low = split_dot(feats[...], cross_down[...])
    low_high = low.astype(BF)
    low_rest = (low - low_high.astype(F32)).astype(BF)
    copies[4].wait()
    copies[5].wait()
    pre_one = None
    for k in range(TABLES + 1):
        scale = dot(low_high, cross_up[:, cols(k)]) + dot(low_rest, cross_up[:, cols(k)])
        scaled[:, cols(k)] = scale
        feat = feats[:, cols(k)]
        term = split_dot(feat * scale + feat, w_top1[cols(k), :])
        pre_one = term if pre_one is None else pre_one + term
    copies[6].wait()
    sig_one = jax.nn.sigmoid(pre_one)
    pre_two = split_dot(pre_one * sig_one, w_top2[...])
    sig_two = jax.nn.sigmoid(pre_two)
    head = w_out[...]
    logits = jnp.sum(pre_two * sig_two * head, axis=1, keepdims=True)
    logits_out[...] = logits
    logit_grad = (jax.nn.sigmoid(logits) - labels[...].astype(F32)) * (1.0 / 32.0)
    grad_two = (logit_grad * head * silu_slope(pre_two, sig_two)).astype(BF)
    grad_one = (dot_nt(grad_two, w_top2[...]) * silu_slope(pre_one, sig_one)).astype(BF)
    low_grad = None
    for k in range(TABLES + 1):
        part = dot_nt(grad_one, w_top1[cols(k), :])
        term = dot_nt((part * feats[:, cols(k)]).astype(BF), cross_up[:, cols(k)])
        low_grad = term if low_grad is None else low_grad + term
        if k > 0:
            scaled[:, cols(k)] = part * (scaled[:, cols(k)] + 1.0)
    low_grad = low_grad.astype(BF)
    for t in range(TABLES):
        back = dot_nt(low_grad, cross_down[cols(t + 1), :])
        emb_grad[t] = (scaled[:, cols(t + 1)] + back).astype(BF)

    to = lax.broadcasted_iota(jnp.int32, (LOOK, LOOK), 0)
    at = lax.broadcasted_iota(jnp.int32, (LOOK, LOOK), 1)
    source = to - to % 16 + ((my_yh + YH - to // 4 % YH) % YH) * 4 + to % 4
    turned = (at == source).astype(BF)

    def one_shard(m, carry):
        picked = dot_nt(turned, counts[m]).astype(BF)
        terms = dot(picked, emb_grad[table_of[m]]).astype(BF)
        for c in range(CORES):
            for x in range(X):
                at = (c * X + x) * 16
                grads[c, x, m % YL, m // YL] = terms[at : at + 16]
        return carry

    lax.fori_loop(0, SHARDS, one_shard, 0, unroll=4)


def run_step(place, table_of, small, large):
    smem = pl.BlockSpec(memory_space=pltpu.SMEM)
    vmem = pl.BlockSpec(memory_space=pltpu.VMEM)
    hbm = pl.BlockSpec(memory_space=pl.ANY)
    counts, own, _, *weights = large
    return pl.pallas_call(
        step_kernel,
        out_shape=(
            jax.ShapeDtypeStruct((CORES, X, YL, Z, 16, E), BF),
            jax.ShapeDtypeStruct((N, 1), F32),
        ),
        in_specs=[smem, smem] + [vmem] * len(small) + [hbm] * len(large),
        out_specs=(vmem, vmem),
        scratch_shapes=[
            pltpu.VMEM(counts.shape, BF),
            pltpu.VMEM((CORES, *own.shape), BF),
            *[pltpu.VMEM(w.shape, BF) for w in weights],
            pltpu.VMEM((N, (TABLES + 1) * E), F32),
            pltpu.VMEM((N, (TABLES + 1) * E), F32),
            pltpu.VMEM((TABLES, N, E), BF),
            pltpu.SMEM((SHARDS,), jnp.int32),
            pltpu.SMEM((TABLES,), jnp.int32),
            pltpu.SemaphoreType.DMA((len(large),)),
        ],
        compiler_params=pltpu.CompilerParams(vmem_limit_bytes=60 * 2**20),
        cost_estimate=pl.CostEstimate(
            flops=4 * 10**9, bytes_accessed=12 * 2**20, transcendentals=2 * 10**5
        ),
    )(place, table_of, *small, *large)


def lanes_kernel(place, counts, out):
    my_yh = place[1]
    at = lax.broadcasted_iota(jnp.int32, (LOOK, LOOK), 0)
    to = lax.broadcasted_iota(jnp.int32, (LOOK, LOOK), 1)
    yh = (my_yh + YH - to // 4 % YH) % YH
    source = (to // 16 % X) * 32 + yh * 8 + (to // 64) * 4 + to % 4
    turned = (at == source).astype(BF)
    out[...] = dot(counts[...].astype(F32).astype(BF), turned).astype(BF)


def turn_lanes(place, counts):
    rows = counts.shape[0] // 8
    return pl.pallas_call(
        lanes_kernel,
        out_shape=jax.ShapeDtypeStruct(counts.shape, BF),
        grid=(8,),
        in_specs=[
            pl.BlockSpec(memory_space=pltpu.SMEM),
            pl.BlockSpec((rows, LOOK), lambda i: (i, 0)),
        ],
        out_specs=pl.BlockSpec((rows, LOOK), lambda i: (i, 0)),
        cost_estimate=pl.CostEstimate(
            flops=2 * 10**8, bytes_accessed=3 * 2**20, transcendentals=0
        ),
    )(place, counts)


def pair_kernel(halves, out):
    def one_block(i, carry):
        at = pl.ds(i * 256, 256)
        out[at] = (halves[0, at].astype(F32) + halves[1, at].astype(F32)).astype(BF)
        return carry

    lax.fori_loop(0, out.shape[0] // 256, one_block, 0, unroll=2)


def sum_kernel(parts, out):
    to = lax.broadcasted_iota(jnp.int32, (E, E), 0)
    at = lax.broadcasted_iota(jnp.int32, (E, E), 1)
    turned = (at == (to // 4 % Z) * 16 + (to // 64) * 4 + to % 4).astype(BF)
    total = parts[0].astype(F32)
    for i in range(1, parts.shape[0]):
        total = total + parts[i].astype(F32)
    out[...] = dot(turned, total.astype(BF)).astype(BF)


def fold(kernel, parts):
    return pl.pallas_call(
        kernel,
        out_shape=jax.ShapeDtypeStruct(parts.shape[1:], BF),
        in_specs=[pl.BlockSpec(memory_space=pltpu.VMEM)],
        out_specs=pl.BlockSpec(memory_space=pltpu.VMEM),
        compiler_params=pltpu.CompilerParams(vmem_limit_bytes=12 * 2**20),
        cost_estimate=pl.CostEstimate(
            flops=5 * 10**7, bytes_accessed=3 * 2**20, transcendentals=0
        ),
    )(parts)


def swap(value, axes):
    return lax.all_to_all(value, axes, split_axis=0, concat_axis=0, tiled=True)


def add_up(value):
    return jnp.sum(value.astype(F32), axis=0)


def turn(value, axis, size, shift):
    return lax.ppermute(value, axis, [(i, (i + shift) % size) for i in range(size)])


def shards(
    table,
    row_ids,
    pool_counts,
    table_of,
    dense_feat,
    labels,
    w_bottom1,
    w_bottom2,
    cross_down,
    cross_up,
    w_top1,
    w_top2,
    w_out,
):
    my_x, my_yh, my_c = lax.axis_index("x"), lax.axis_index("yh"), lax.axis_index("c")
    place = jnp.stack([my_x, my_yh, my_c]).astype(jnp.int32)
    first = ((my_x * YH + my_yh) * CORES + my_c) * 4
    ids = lax.dynamic_slice(row_ids, (0, first), (1, 4))[0]
    mine = jnp.take(table, ids, axis=0, mode="clip").astype(BF)
    mine = jnp.broadcast_to(mine, (SHARDS, 4, E))
    mine, pool_counts = lax.optimization_barrier((mine, pool_counts))
    looked = swap(mine, MP)
    counts = turn_lanes(place, pool_counts).reshape(SHARDS, N, LOOK)
    looked, counts = lax.optimization_barrier((looked, counts))
    counts = swap(counts, MP)
    looked = jnp.concatenate(
        [looked] + [turn(looked, "yh", YH, k) for k in range(1, YH)], axis=1
    )
    looked = jnp.stack([looked] + [turn(looked, "x", X, k) for k in range(1, X)])
    others = turn(looked, "c", CORES, 1)

    hidden = lax.dot_general(
        dense_feat, w_bottom1, (((0,), (0,)), ((), ())), preferred_element_type=F32
    )
    hidden = jax.nn.relu(hidden).astype(BF)
    bottom = jax.nn.relu(dot(hidden, w_bottom2)).astype(BF)

    grads, logits = run_step(
        place,
        table_of,
        (bottom, labels.reshape(N, 1), w_out.reshape(1, -1)),
        (counts, looked, others, cross_down, cross_up, w_top1, w_top2),
    )
    grads = swap(grads.reshape(CORES, X * YL * Z * 16, E), "c")
    grads = fold(pair_kernel, grads).reshape(X * YL, Z * 16, E)
    grads = fold(sum_kernel, swap(grads, ("x", "yl"))).reshape(YH * Z, 4, E)
    grads = add_up(swap(grads, ("yh", "z")))
    return grads, logits.reshape(N)


def solution(mesh):
    fine = Mesh(mesh.devices.reshape(X, YH, CORES, Z, YL), REP + MP)
    both = REP + MP
    return jax.shard_map(
        shards,
        mesh=fine,
        in_specs=(
            P(MP, None),
            P(MP, None),
            P(REP, MP),
            P(),
            P(None, both),
            P(both),
            P(),
            P(),
            P(),
            P(),
            P(),
            P(),
            P(),
        ),
        out_specs=(P(REP, MP), P(both)),
        check_vma=False,
    )
```

```python
import functools

import jax
import jax.numpy as jnp
from jax import lax
from jax.experimental import pallas as pl
from jax.experimental.pallas import tpu as pltpu
from jax.sharding import Mesh
from jax.sharding import PartitionSpec as P

X, YH, CORES, Z, YL = 4, 4, 2, 16, 2
REP = ("x", "yh", "c")
MP = ("z", "yl")
SHARDS = Z * YL
TABLES = 8
PER = SHARDS // TABLES
E = 256
N = 128
LOOK = 128
BF = jnp.bfloat16
F32 = jnp.float32


def silu_slope(value, sig):
    return sig + value * sig * (1.0 - sig)


def dot(a, b):
    return jnp.dot(a, b, preferred_element_type=F32)


def dot_nt(a, b):
    return lax.dot_general(a, b, (((1,), (1,)), ((), ())), preferred_element_type=F32)


def dot_tn(a, b):
    return lax.dot_general(a, b, (((0,), (0,)), ((), ())), preferred_element_type=F32)


def split_dot(value, weights):
    high = value.astype(BF)
    low = (value - high.astype(F32)).astype(BF)
    return dot(high, weights) + dot(low, weights)


def cols(k):
    return slice(k * E, (k + 1) * E)


WIDE = (TABLES + 1) * E
TOP = 512
PIECES = ((0, WIDE), (WIDE, WIDE), (2 * WIDE, 2 * WIDE), (4 * WIDE, 2 * TOP))
PACKED = 4 * WIDE + 2 * TOP


def step_kernel(
    place,
    table_of,
    bottom,
    labels,
    w_out,
    counts,
    own,
    other,
    packed_hbm,
    grads,
    logits_out,
    packed,
    feats,
    scaled,
    emb_grad,
    order,
    filled,
    arrived,
):
    copies = [
        pltpu.make_async_copy(
            packed_hbm.at[pl.ds(first, rows)], packed.at[pl.ds(first, rows)], arrived.at[i]
        )
        for i, (first, rows) in enumerate(PIECES)
    ]
    for copy in copies:
        copy.start()
    my_x, my_c = place[0], place[2]

    def down(k):
        return packed[cols(k), :]

    def up(k):
        return packed[cols(TABLES + 1 + k), :]

    def top1(k, half):
        return packed[cols((2 + half) * (TABLES + 1) + k), :]

    def top2(half):
        return packed[4 * WIDE + half * TOP : 4 * WIDE + (half + 1) * TOP, :]

    for t in range(TABLES):
        filled[t] = 0
    for m in range(SHARDS):
        t = table_of[m]
        k = filled[t]
        order[t * PER + k] = m
        filled[t] = k + 1

    feats[:, cols(0)] = bottom[...].astype(F32)
    for t in range(TABLES):
        acc = None
        for k in range(PER):
            m = order[t * PER + k]
            turns = [lax.rem(my_x + X - x, X) for x in range(X)]
            near = [own[k_x, m] for k_x in turns]
            far = [other[k_x, m] for k_x in turns]
            rows = jnp.concatenate(
                [jnp.where(my_c == 0, a, b) for a, b in zip(near, far)]
                + [jnp.where(my_c == 0, b, a) for a, b in zip(near, far)],
                axis=0,
            )
            term = dot(counts[m], rows)
            acc = term if acc is None else acc + term
        feats[:, cols(t + 1)] = acc

    copies[0].wait()
    low = split_dot(feats[...], packed[0:WIDE, :])
    low_high = low.astype(BF)
    low_rest = (low - low_high.astype(F32)).astype(BF)
    copies[1].wait()
    copies[2].wait()
    pre_one = [None, None]
    for k in range(TABLES + 1):
        scale = dot(low_high, up(k)) + dot(low_rest, up(k))
        scaled[:, cols(k)] = scale
        feat = feats[:, cols(k)]
        crossed = feat * scale + feat
        for half in range(2):
            term = split_dot(crossed, top1(k, half))
            pre_one[half] = term if k == 0 else pre_one[half] + term
    pre_one = jnp.concatenate(pre_one, axis=1)
    copies[3].wait()
    sig_one = jax.nn.sigmoid(pre_one)
    act_one = pre_one * sig_one
    pre_two = jnp.concatenate([split_dot(act_one, top2(0)), split_dot(act_one, top2(1))], axis=1)
    sig_two = jax.nn.sigmoid(pre_two)
    head = w_out[...]
    logits = jnp.sum(pre_two * sig_two * head, axis=1, keepdims=True)
    logits_out[...] = logits
    logit_grad = (jax.nn.sigmoid(logits) - labels[...].astype(F32)) * (1.0 / 32.0)
    grad_two = (logit_grad * head * silu_slope(pre_two, sig_two)).astype(BF)
    grad_act = dot_nt(grad_two[:, cols(0)], top2(0)) + dot_nt(grad_two[:, cols(1)], top2(1))
    grad_one = (grad_act * silu_slope(pre_one, sig_one)).astype(BF)
    low_grad = None
    for k in range(TABLES + 1):
        part = dot_nt(grad_one[:, cols(0)], top1(k, 0)) + dot_nt(grad_one[:, cols(1)], top1(k, 1))
        term = dot_nt((part * feats[:, cols(k)]).astype(BF), up(k))
        low_grad = term if low_grad is None else low_grad + term
        if k > 0:
            scaled[:, cols(k)] = part * (scaled[:, cols(k)] + 1.0)
    low_grad = low_grad.astype(BF)
    for t in range(TABLES):
        back = dot_nt(low_grad, down(t + 1))
        emb_grad[t] = (scaled[:, cols(t + 1)] + back).astype(BF)

    def one_shard(m, carry):
        terms = dot_tn(counts[m], emb_grad[table_of[m]]).astype(BF)
        for c in range(CORES):
            for x in range(X):
                at = (c * X + x) * 16
                grads[c, x, m % YL, m // YL] = terms[at : at + 16]
        return carry

    lax.fori_loop(0, SHARDS, one_shard, 0, unroll=8)


def run_step(place, table_of, small, packed):
    smem = pl.BlockSpec(memory_space=pltpu.SMEM)
    vmem = pl.BlockSpec(memory_space=pltpu.VMEM)
    hbm = pl.BlockSpec(memory_space=pl.ANY)
    return pl.pallas_call(
        step_kernel,
        out_shape=(
            jax.ShapeDtypeStruct((CORES, X, YL, Z, 16, E), BF),
            jax.ShapeDtypeStruct((N, 1), F32),
        ),
        in_specs=[smem, smem] + [vmem] * len(small) + [hbm],
        out_specs=(vmem, vmem),
        scratch_shapes=[
            pltpu.VMEM((PACKED, E), BF),
            pltpu.VMEM((N, (TABLES + 1) * E), F32),
            pltpu.VMEM((N, (TABLES + 1) * E), F32),
            pltpu.VMEM((TABLES, N, E), BF),
            pltpu.SMEM((SHARDS,), jnp.int32),
            pltpu.SMEM((TABLES,), jnp.int32),
            pltpu.SemaphoreType.DMA((len(PIECES),)),
        ],
        compiler_params=pltpu.CompilerParams(vmem_limit_bytes=46 * 2**20),
        cost_estimate=pl.CostEstimate(
            flops=4 * 10**9, bytes_accessed=12 * 2**20, transcendentals=2 * 10**5
        ),
    )(place, table_of, *small, packed)


def pack_kernel(down, up, top1, top2, packed, arrived):
    moves = [(down, 0)]
    moves += [(up.at[:, pl.ds(k * E, E)], WIDE + k * E) for k in range(TABLES + 1)]
    moves += [(top1.at[:, pl.ds(h * E, E)], (2 + h) * WIDE) for h in range(2)]
    moves += [(top2.at[:, pl.ds(h * E, E)], 4 * WIDE + h * TOP) for h in range(2)]
    copies = [
        pltpu.make_async_copy(source, packed.at[pl.ds(first, source.shape[0])], arrived.at[i])
        for i, (source, first) in enumerate(moves)
    ]
    for copy in copies:
        copy.start()
    for copy in copies:
        copy.wait()


def pack(*weights):
    anywhere = pl.BlockSpec(memory_space=pl.ANY)
    return pl.pallas_call(
        pack_kernel,
        out_shape=jax.ShapeDtypeStruct((PACKED, E), BF),
        in_specs=[anywhere] * len(weights),
        out_specs=anywhere,
        scratch_shapes=[pltpu.SemaphoreType.DMA((TABLES + 6,))],
        cost_estimate=pl.CostEstimate(flops=0, bytes_accessed=10 * 2**20, transcendentals=0),
    )(*weights)


def lanes_kernel(place, counts, out):
    my_yh = place[1]
    at = lax.broadcasted_iota(jnp.int32, (LOOK, LOOK), 0)
    to = lax.broadcasted_iota(jnp.int32, (LOOK, LOOK), 1)
    yh = (my_yh + YH - to // 4 % YH) % YH
    source = (to // 16 % X) * 32 + yh * 8 + (to // 64) * 4 + to % 4
    turned = (at == source).astype(BF)
    out[...] = dot(counts[...].astype(F32).astype(BF), turned).astype(BF)


def turn_lanes(place, counts):
    rows = counts.shape[0] // 8
    return pl.pallas_call(
        lanes_kernel,
        out_shape=jax.ShapeDtypeStruct(counts.shape, BF),
        grid=(8,),
        in_specs=[
            pl.BlockSpec(memory_space=pltpu.SMEM),
            pl.BlockSpec((rows, LOOK), lambda i: (i, 0)),
        ],
        out_specs=pl.BlockSpec((rows, LOOK), lambda i: (i, 0)),
        cost_estimate=pl.CostEstimate(
            flops=2 * 10**8, bytes_accessed=3 * 2**20, transcendentals=0
        ),
    )(place, counts)


def pair_kernel(_, halves, out):
    def one_block(i, carry):
        at = pl.ds(i * 256, 256)
        out[at] = (halves[0, at].astype(F32) + halves[1, at].astype(F32)).astype(BF)
        return carry

    lax.fori_loop(0, out.shape[0] // 256, one_block, 0, unroll=2)


def sum_kernel(place, parts, out):
    to = lax.broadcasted_iota(jnp.int32, (E, E), 0)
    at = lax.broadcasted_iota(jnp.int32, (E, E), 1)
    back = (place[1] + YH - to // 64) % YH
    turned = (at == (to // 4 % Z) * 16 + back * 4 + to % 4).astype(BF)
    total = parts[0].astype(F32)
    for i in range(1, parts.shape[0]):
        total = total + parts[i].astype(F32)
    out[...] = dot(turned, total.astype(BF)).astype(BF)


def fold(kernel, place, parts):
    return pl.pallas_call(
        kernel,
        out_shape=jax.ShapeDtypeStruct(parts.shape[1:], BF),
        in_specs=[
            pl.BlockSpec(memory_space=pltpu.SMEM),
            pl.BlockSpec(memory_space=pltpu.VMEM),
        ],
        out_specs=pl.BlockSpec(memory_space=pltpu.VMEM),
        compiler_params=pltpu.CompilerParams(vmem_limit_bytes=12 * 2**20),
        cost_estimate=pl.CostEstimate(
            flops=5 * 10**7, bytes_accessed=3 * 2**20, transcendentals=0
        ),
    )(place, parts)


def swap(value, axes):
    return lax.all_to_all(value, axes, split_axis=0, concat_axis=0, tiled=True)


def add_up(value):
    return jnp.sum(value.astype(F32), axis=0)


def turn(value, axis, size, shift):
    return lax.ppermute(value, axis, [(i, (i + shift) % size) for i in range(size)])


def shards(
    table,
    row_ids,
    pool_counts,
    table_of,
    dense_feat,
    labels,
    w_bottom1,
    w_bottom2,
    cross_down,
    cross_up,
    w_top1,
    w_top2,
    w_out,
):
    my_x, my_yh, my_c = lax.axis_index("x"), lax.axis_index("yh"), lax.axis_index("c")
    place = jnp.stack([my_x, my_yh, my_c]).astype(jnp.int32)
    first = ((my_x * YH + my_yh) * CORES + my_c) * 4
    ids = lax.dynamic_slice(row_ids, (0, first), (1, 4))[0]
    mine = jnp.take(table, ids, axis=0, mode="clip").astype(BF)
    mine = jnp.broadcast_to(mine, (SHARDS, 4, E))
    mine, pool_counts = lax.optimization_barrier((mine, pool_counts))
    looked = swap(mine, MP)
    counts = turn_lanes(place, pool_counts).reshape(SHARDS, N, LOOK)
    looked, counts = lax.optimization_barrier((looked, counts))
    counts = swap(counts, MP)
    looked = jnp.concatenate(
        [looked] + [turn(looked, "yh", YH, k) for k in range(1, YH)], axis=1
    )
    looked, *weights = lax.optimization_barrier((looked, cross_down, cross_up, w_top1, w_top2))
    packed = pack(*weights)
    looked = jnp.stack([looked] + [turn(looked, "x", X, k) for k in range(1, X)])
    others = turn(looked, "c", CORES, 1)

    hidden = lax.dot_general(
        dense_feat, w_bottom1, (((0,), (0,)), ((), ())), preferred_element_type=F32
    )
    hidden = jax.nn.relu(hidden).astype(BF)
    bottom = jax.nn.relu(dot(hidden, w_bottom2)).astype(BF)

    grads, logits = run_step(
        place,
        table_of,
        (bottom, labels.reshape(N, 1), w_out.reshape(1, -1), counts, looked, others),
        packed,
    )
    grads = swap(grads.reshape(CORES, X * YL * Z * 16, E), "c")
    grads = fold(pair_kernel, place, grads).reshape(X * YL, Z * 16, E)
    grads = fold(sum_kernel, place, swap(grads, ("x", "yl"))).reshape(YH * Z, 4, E)
    grads = add_up(swap(grads, ("yh", "z")))
    return grads, logits.reshape(N)


def solution(mesh):
    fine = Mesh(mesh.devices.reshape(X, YH, CORES, Z, YL), REP + MP)
    both = REP + MP
    return jax.shard_map(
        shards,
        mesh=fine,
        in_specs=(
            P(MP, None),
            P(MP, None),
            P(REP, MP),
            P(),
            P(None, both),
            P(both),
            P(),
            P(),
            P(),
            P(),
            P(),
            P(),
            P(),
        ),
        out_specs=(P(REP, MP), P(both)),
        check_vma=False,
    )
```

```python
import functools

import jax
import jax.numpy as jnp
from jax import lax
from jax.experimental import pallas as pl
from jax.experimental.pallas import tpu as pltpu
from jax.sharding import Mesh
from jax.sharding import PartitionSpec as P

X, YH, CORES, Z, YL = 4, 4, 2, 16, 2
REP = ("x", "yh", "c")
MP = ("z", "yl")
SHARDS = Z * YL
TABLES = 8
PER = SHARDS // TABLES
E = 256
N = 128
LOOK = 128
BF = jnp.bfloat16
F32 = jnp.float32


def silu_slope(value, sig):
    return sig + value * sig * (1.0 - sig)


def dot(a, b):
    return jnp.dot(a, b, preferred_element_type=F32)


def dot_nt(a, b):
    return lax.dot_general(a, b, (((1,), (1,)), ((), ())), preferred_element_type=F32)


def dot_tn(a, b):
    return lax.dot_general(a, b, (((0,), (0,)), ((), ())), preferred_element_type=F32)


def split_dot(value, weights):
    high = value.astype(BF)
    low = (value - high.astype(F32)).astype(BF)
    return dot(high, weights) + dot(low, weights)


def cols(k):
    return slice(k * E, (k + 1) * E)


WIDE = (TABLES + 1) * E
TOP = 512
PIECES = ((0, WIDE), (WIDE, WIDE), (2 * WIDE, 2 * WIDE), (4 * WIDE, 2 * TOP))
PACKED = 4 * WIDE + 2 * TOP


def step_kernel(
    place,
    table_of,
    bottom,
    labels,
    w_out,
    counts,
    own,
    other,
    packed_hbm,
    grads,
    logits_out,
    packed,
    feats,
    scaled,
    emb_grad,
    order,
    filled,
    arrived,
):
    copies = [
        pltpu.make_async_copy(
            packed_hbm.at[pl.ds(first, rows)], packed.at[pl.ds(first, rows)], arrived.at[i]
        )
        for i, (first, rows) in enumerate(PIECES)
    ]
    for copy in copies:
        copy.start()
    my_x, my_c = place[0], place[2]

    def down(k):
        return packed[cols(k), :]

    def up(k):
        return packed[cols(TABLES + 1 + k), :]

    def top1(k, half):
        return packed[cols((2 + half) * (TABLES + 1) + k), :]

    def top2(half):
        return packed[4 * WIDE + half * TOP : 4 * WIDE + (half + 1) * TOP, :]

    for t in range(TABLES):
        filled[t] = 0
    for m in range(SHARDS):
        t = table_of[m]
        k = filled[t]
        order[t * PER + k] = m
        filled[t] = k + 1

    feats[:, cols(0)] = bottom[...].astype(F32)
    for t in range(TABLES):
        acc = None
        for k in range(PER):
            m = order[t * PER + k]
            turns = [lax.rem(my_x + X - x, X) for x in range(X)]
            near = [own[k_x, m] for k_x in turns]
            far = [other[k_x, m] for k_x in turns]
            rows = jnp.concatenate(
                [jnp.where(my_c == 0, a, b) for a, b in zip(near, far)]
                + [jnp.where(my_c == 0, b, a) for a, b in zip(near, far)],
                axis=0,
            )
            term = dot(counts[m], rows)
            acc = term if acc is None else acc + term
        feats[:, cols(t + 1)] = acc

    copies[0].wait()
    low = split_dot(feats[...], packed[0:WIDE, :])
    low_high = low.astype(BF)
    low_rest = (low - low_high.astype(F32)).astype(BF)
    copies[1].wait()
    copies[2].wait()
    pre_one = [None, None]
    for k in range(TABLES + 1):
        scale = dot(low_high, up(k)) + dot(low_rest, up(k))
        scaled[:, cols(k)] = scale
        feat = feats[:, cols(k)]
        crossed = feat * scale + feat
        for half in range(2):
            term = split_dot(crossed, top1(k, half))
            pre_one[half] = term if k == 0 else pre_one[half] + term
    pre_one = jnp.concatenate(pre_one, axis=1)
    copies[3].wait()
    sig_one = jax.nn.sigmoid(pre_one)
    act_one = pre_one * sig_one
    pre_two = jnp.concatenate([split_dot(act_one, top2(0)), split_dot(act_one, top2(1))], axis=1)
    sig_two = jax.nn.sigmoid(pre_two)
    head = w_out[...]
    logits = jnp.sum(pre_two * sig_two * head, axis=1, keepdims=True)
    logits_out[...] = logits
    logit_grad = (jax.nn.sigmoid(logits) - labels[...].astype(F32)) * (1.0 / 32.0)
    grad_two = (logit_grad * head * silu_slope(pre_two, sig_two)).astype(BF)
    grad_act = dot_nt(grad_two[:, cols(0)], top2(0)) + dot_nt(grad_two[:, cols(1)], top2(1))
    grad_one = (grad_act * silu_slope(pre_one, sig_one)).astype(BF)
    low_grad = None
    for k in range(TABLES + 1):
        part = dot_nt(grad_one[:, cols(0)], top1(k, 0)) + dot_nt(grad_one[:, cols(1)], top1(k, 1))
        term = dot_nt((part * feats[:, cols(k)]).astype(BF), up(k))
        low_grad = term if low_grad is None else low_grad + term
        if k > 0:
            scaled[:, cols(k)] = part * (scaled[:, cols(k)] + 1.0)
    low_grad = low_grad.astype(BF)
    for t in range(TABLES):
        back = dot_nt(low_grad, down(t + 1))
        emb_grad[t] = (scaled[:, cols(t + 1)] + back).astype(BF)

    def one_shard(m, carry):
        terms = dot_tn(counts[m], emb_grad[table_of[m]]).astype(BF)
        for c in range(CORES):
            for x in range(X):
                at = (c * X + x) * 16
                grads[c, x, m % YL, m // YL] = terms[at : at + 16]
        return carry

    lax.fori_loop(0, SHARDS, one_shard, 0, unroll=8)


def run_step(place, table_of, small, packed):
    smem = pl.BlockSpec(memory_space=pltpu.SMEM)
    vmem = pl.BlockSpec(memory_space=pltpu.VMEM)
    hbm = pl.BlockSpec(memory_space=pl.ANY)
    return pl.pallas_call(
        step_kernel,
        out_shape=(
            jax.ShapeDtypeStruct((CORES, X, YL, Z, 16, E), BF),
            jax.ShapeDtypeStruct((N, 1), F32),
        ),
        in_specs=[smem, smem] + [vmem] * len(small) + [hbm],
        out_specs=(vmem, vmem),
        scratch_shapes=[
            pltpu.VMEM((PACKED, E), BF),
            pltpu.VMEM((N, (TABLES + 1) * E), F32),
            pltpu.VMEM((N, (TABLES + 1) * E), F32),
            pltpu.VMEM((TABLES, N, E), BF),
            pltpu.SMEM((SHARDS,), jnp.int32),
            pltpu.SMEM((TABLES,), jnp.int32),
            pltpu.SemaphoreType.DMA((len(PIECES),)),
        ],
        compiler_params=pltpu.CompilerParams(vmem_limit_bytes=46 * 2**20),
        cost_estimate=pl.CostEstimate(
            flops=4 * 10**9, bytes_accessed=12 * 2**20, transcendentals=2 * 10**5
        ),
    )(place, table_of, *small, packed)


def pack_kernel(down, up, top1, top2, packed_hbm, packed, arrived):
    moves = [(down, 0)]
    moves += [(up.at[:, pl.ds(k * E, E)], WIDE + k * E) for k in range(TABLES + 1)]
    moves += [(top1.at[:, pl.ds(h * E, E)], (2 + h) * WIDE) for h in range(2)]
    moves += [(top2.at[:, pl.ds(h * E, E)], 4 * WIDE + h * TOP) for h in range(2)]
    copies = [
        pltpu.make_async_copy(source, packed.at[pl.ds(first, source.shape[0])], arrived.at[i])
        for i, (source, first) in enumerate(moves)
    ]
    for copy in copies:
        copy.start()
    for copy in copies:
        copy.wait()
    result = pltpu.make_async_copy(packed, packed_hbm, arrived.at[len(moves)])
    result.start()
    result.wait()


def pack(*weights):
    anywhere = pl.BlockSpec(memory_space=pl.ANY)
    return pl.pallas_call(
        pack_kernel,
        out_shape=jax.ShapeDtypeStruct((PACKED, E), BF),
        in_specs=[anywhere] * len(weights),
        out_specs=anywhere,
        scratch_shapes=[
            pltpu.VMEM((PACKED, E), BF),
            pltpu.SemaphoreType.DMA((TABLES + 7,)),
        ],
        compiler_params=pltpu.CompilerParams(vmem_limit_bytes=12 * 2**20),
        cost_estimate=pl.CostEstimate(flops=0, bytes_accessed=10 * 2**20, transcendentals=0),
    )(*weights)


def lanes_kernel(place, counts, out):
    my_yh = place[1]
    at = lax.broadcasted_iota(jnp.int32, (LOOK, LOOK), 0)
    to = lax.broadcasted_iota(jnp.int32, (LOOK, LOOK), 1)
    yh = (my_yh + YH - to // 4 % YH) % YH
    source = (to // 16 % X) * 32 + yh * 8 + (to // 64) * 4 + to % 4
    turned = (at == source).astype(BF)
    out[...] = dot(counts[...].astype(F32).astype(BF), turned).astype(BF)


def turn_lanes(place, counts):
    rows = counts.shape[0] // 8
    return pl.pallas_call(
        lanes_kernel,
        out_shape=jax.ShapeDtypeStruct(counts.shape, BF),
        grid=(8,),
        in_specs=[
            pl.BlockSpec(memory_space=pltpu.SMEM),
            pl.BlockSpec((rows, LOOK), lambda i: (i, 0)),
        ],
        out_specs=pl.BlockSpec((rows, LOOK), lambda i: (i, 0)),
        cost_estimate=pl.CostEstimate(
            flops=2 * 10**8, bytes_accessed=3 * 2**20, transcendentals=0
        ),
    )(place, counts)


def pair_kernel(_, halves, out):
    def one_block(i, carry):
        at = pl.ds(i * 256, 256)
        out[at] = (halves[0, at].astype(F32) + halves[1, at].astype(F32)).astype(BF)
        return carry

    lax.fori_loop(0, out.shape[0] // 256, one_block, 0, unroll=2)


def sum_kernel(place, parts, out):
    to = lax.broadcasted_iota(jnp.int32, (E, E), 0)
    at = lax.broadcasted_iota(jnp.int32, (E, E), 1)
    back = (place[1] + YH - to // 64) % YH
    turned = (at == (to // 4 % Z) * 16 + back * 4 + to % 4).astype(BF)
    total = parts[0].astype(F32)
    for i in range(1, parts.shape[0]):
        total = total + parts[i].astype(F32)
    out[...] = dot(turned, total.astype(BF)).astype(BF)


def fold(kernel, place, parts):
    return pl.pallas_call(
        kernel,
        out_shape=jax.ShapeDtypeStruct(parts.shape[1:], BF),
        in_specs=[
            pl.BlockSpec(memory_space=pltpu.SMEM),
            pl.BlockSpec(memory_space=pltpu.VMEM),
        ],
        out_specs=pl.BlockSpec(memory_space=pltpu.VMEM),
        compiler_params=pltpu.CompilerParams(vmem_limit_bytes=12 * 2**20),
        cost_estimate=pl.CostEstimate(
            flops=5 * 10**7, bytes_accessed=3 * 2**20, transcendentals=0
        ),
    )(place, parts)


def swap(value, axes):
    return lax.all_to_all(value, axes, split_axis=0, concat_axis=0, tiled=True)


def add_up(value):
    return jnp.sum(value.astype(F32), axis=0)


def turn(value, axis, size, shift):
    return lax.ppermute(value, axis, [(i, (i + shift) % size) for i in range(size)])


def shards(
    table,
    row_ids,
    pool_counts,
    table_of,
    dense_feat,
    labels,
    w_bottom1,
    w_bottom2,
    cross_down,
    cross_up,
    w_top1,
    w_top2,
    w_out,
):
    my_x, my_yh, my_c = lax.axis_index("x"), lax.axis_index("yh"), lax.axis_index("c")
    place = jnp.stack([my_x, my_yh, my_c]).astype(jnp.int32)
    first = ((my_x * YH + my_yh) * CORES + my_c) * 4
    ids = lax.dynamic_slice(row_ids, (0, first), (1, 4))[0]
    mine = jnp.take(table, ids, axis=0, mode="clip").astype(BF)
    mine = jnp.broadcast_to(mine, (SHARDS, 4, E))
    mine, pool_counts = lax.optimization_barrier((mine, pool_counts))
    looked = swap(mine, MP)
    counts = turn_lanes(place, pool_counts).reshape(SHARDS, N, LOOK)
    looked, counts = lax.optimization_barrier((looked, counts))
    counts = swap(counts, MP)
    looked = jnp.concatenate(
        [looked] + [turn(looked, "yh", YH, k) for k in range(1, YH)], axis=1
    )
    looked, *weights = lax.optimization_barrier((looked, cross_down, cross_up, w_top1, w_top2))
    packed = pack(*weights)
    looked = jnp.stack([looked] + [turn(looked, "x", X, k) for k in range(1, X)])
    others = turn(looked, "c", CORES, 1)

    hidden = lax.dot_general(
        dense_feat, w_bottom1, (((0,), (0,)), ((), ())), preferred_element_type=F32
    )
    hidden = jax.nn.relu(hidden).astype(BF)
    bottom = jax.nn.relu(dot(hidden, w_bottom2)).astype(BF)

    grads, logits = run_step(
        place,
        table_of,
        (bottom, labels.reshape(N, 1), w_out.reshape(1, -1), counts, looked, others),
        packed,
    )
    grads = swap(grads.reshape(CORES, X * YL * Z * 16, E), "c")
    grads = fold(pair_kernel, place, grads).reshape(X * YL, Z * 16, E)
    grads = fold(sum_kernel, place, swap(grads, ("x", "yl"))).reshape(YH * Z, 4, E)
    grads = add_up(swap(grads, ("yh", "z")))
    return grads, logits.reshape(N)


def solution(mesh):
    fine = Mesh(mesh.devices.reshape(X, YH, CORES, Z, YL), REP + MP)
    both = REP + MP
    return jax.shard_map(
        shards,
        mesh=fine,
        in_specs=(
            P(MP, None),
            P(MP, None),
            P(REP, MP),
            P(),
            P(None, both),
            P(both),
            P(),
            P(),
            P(),
            P(),
            P(),
            P(),
            P(),
        ),
        out_specs=(P(REP, MP), P(both)),
        check_vma=False,
    )
```

```python
import functools

import jax
import jax.numpy as jnp
from jax import lax
from jax.experimental import pallas as pl
from jax.experimental.pallas import tpu as pltpu
from jax.sharding import Mesh
from jax.sharding import PartitionSpec as P

X, YH, CORES, Z, YL = 4, 4, 2, 16, 2
REP = ("x", "yh", "c")
MP = ("z", "yl")
SHARDS = Z * YL
TABLES = 8
PER = SHARDS // TABLES
E = 256
N = 128
LOOK = 128
BF = jnp.bfloat16
F32 = jnp.float32


def silu_slope(value, sig):
    return sig + value * sig * (1.0 - sig)


def dot(a, b):
    return jnp.dot(a, b, preferred_element_type=F32)


def dot_nt(a, b):
    return lax.dot_general(a, b, (((1,), (1,)), ((), ())), preferred_element_type=F32)


def dot_tn(a, b):
    return lax.dot_general(a, b, (((0,), (0,)), ((), ())), preferred_element_type=F32)


def split_dot(value, weights):
    high = value.astype(BF)
    low = (value - high.astype(F32)).astype(BF)
    return dot(high, weights) + dot(low, weights)


def cols(k):
    return slice(k * E, (k + 1) * E)


WIDE = (TABLES + 1) * E
TOP = 512
PIECES = ((0, WIDE), (WIDE, WIDE), (2 * WIDE, 2 * WIDE), (4 * WIDE, 2 * TOP))
PACKED = 4 * WIDE + 2 * TOP


def step_kernel(
    place,
    table_of,
    bottom,
    labels,
    w_out,
    counts,
    own,
    other,
    packed_hbm,
    grads,
    logits_out,
    packed,
    feats,
    scaled,
    emb_grad,
    order,
    filled,
    arrived,
):
    copies = [
        pltpu.make_async_copy(
            packed_hbm.at[pl.ds(first, rows)], packed.at[pl.ds(first, rows)], arrived.at[i]
        )
        for i, (first, rows) in enumerate(PIECES)
    ]
    for copy in copies:
        copy.start()
    my_x, my_c = place[0], place[2]

    def down(k):
        return packed[cols(k), :]

    def up(k):
        return packed[cols(TABLES + 1 + k), :]

    def top1(k, half):
        return packed[cols((2 + half) * (TABLES + 1) + k), :]

    def top2(half):
        return packed[4 * WIDE + half * TOP : 4 * WIDE + (half + 1) * TOP, :]

    for t in range(TABLES):
        filled[t] = 0
    for m in range(SHARDS):
        t = table_of[m]
        k = filled[t]
        order[t * PER + k] = m
        filled[t] = k + 1

    feats[:, cols(0)] = bottom[...].astype(F32)
    for t in range(TABLES):
        acc = None
        for k in range(PER):
            m = order[t * PER + k]
            turns = [lax.rem(my_x + X - x, X) for x in range(X)]
            near = [own[k_x, m] for k_x in turns]
            far = [other[k_x, m] for k_x in turns]
            rows = jnp.concatenate(
                [jnp.where(my_c == 0, a, b) for a, b in zip(near, far)]
                + [jnp.where(my_c == 0, b, a) for a, b in zip(near, far)],
                axis=0,
            )
            term = dot(counts[m], rows)
            acc = term if acc is None else acc + term
        feats[:, cols(t + 1)] = acc

    copies[0].wait()
    low = split_dot(feats[...], packed[0:WIDE, :])
    low_high = low.astype(BF)
    low_rest = (low - low_high.astype(F32)).astype(BF)
    copies[1].wait()
    copies[2].wait()
    pre_one = [None, None]
    for k in range(TABLES + 1):
        scale = dot(low_high, up(k)) + dot(low_rest, up(k))
        scaled[:, cols(k)] = scale
        feat = feats[:, cols(k)]
        crossed = feat * scale + feat
        for half in range(2):
            term = split_dot(crossed, top1(k, half))
            pre_one[half] = term if k == 0 else pre_one[half] + term
    pre_one = jnp.concatenate(pre_one, axis=1)
    copies[3].wait()
    sig_one = jax.nn.sigmoid(pre_one)
    act_one = pre_one * sig_one
    pre_two = jnp.concatenate([split_dot(act_one, top2(0)), split_dot(act_one, top2(1))], axis=1)
    sig_two = jax.nn.sigmoid(pre_two)
    head = w_out[...]
    logits = jnp.sum(pre_two * sig_two * head, axis=1, keepdims=True)
    across = lax.broadcasted_iota(jnp.int32, (N, N), 0) == lax.broadcasted_iota(
        jnp.int32, (N, N), 1
    )
    logits_out[...] = jnp.sum(jnp.where(across, logits, 0.0), axis=0, keepdims=True)
    logit_grad = (jax.nn.sigmoid(logits) - labels[...].astype(F32)) * (1.0 / 32.0)
    grad_two = (logit_grad * head * silu_slope(pre_two, sig_two)).astype(BF)
    grad_act = dot_nt(grad_two[:, cols(0)], top2(0)) + dot_nt(grad_two[:, cols(1)], top2(1))
    grad_one = (grad_act * silu_slope(pre_one, sig_one)).astype(BF)
    low_grad = None
    for k in range(TABLES + 1):
        part = dot_nt(grad_one[:, cols(0)], top1(k, 0)) + dot_nt(grad_one[:, cols(1)], top1(k, 1))
        term = dot_nt((part * feats[:, cols(k)]).astype(BF), up(k))
        low_grad = term if low_grad is None else low_grad + term
        if k > 0:
            scaled[:, cols(k)] = part * (scaled[:, cols(k)] + 1.0)
    low_grad = low_grad.astype(BF)
    for t in range(TABLES):
        back = dot_nt(low_grad, down(t + 1))
        emb_grad[t] = (scaled[:, cols(t + 1)] + back).astype(BF)

    def one_shard(m, carry):
        terms = dot_tn(counts[m], emb_grad[table_of[m]]).astype(BF)
        for c in range(CORES):
            for x in range(X):
                at = (c * X + x) * 16
                grads[c, x, m % YL, m // YL] = terms[at : at + 16]
        return carry

    lax.fori_loop(0, SHARDS, one_shard, 0, unroll=8)


def run_step(place, table_of, small, packed):
    smem = pl.BlockSpec(memory_space=pltpu.SMEM)
    vmem = pl.BlockSpec(memory_space=pltpu.VMEM)
    hbm = pl.BlockSpec(memory_space=pl.ANY)
    return pl.pallas_call(
        step_kernel,
        out_shape=(
            jax.ShapeDtypeStruct((CORES, X, YL, Z, 16, E), BF),
            jax.ShapeDtypeStruct((1, N), F32),
        ),
        in_specs=[smem, smem] + [vmem] * len(small) + [hbm],
        out_specs=(vmem, vmem),
        scratch_shapes=[
            pltpu.VMEM((PACKED, E), BF),
            pltpu.VMEM((N, (TABLES + 1) * E), F32),
            pltpu.VMEM((N, (TABLES + 1) * E), F32),
            pltpu.VMEM((TABLES, N, E), BF),
            pltpu.SMEM((SHARDS,), jnp.int32),
            pltpu.SMEM((TABLES,), jnp.int32),
            pltpu.SemaphoreType.DMA((len(PIECES),)),
        ],
        compiler_params=pltpu.CompilerParams(vmem_limit_bytes=46 * 2**20),
        cost_estimate=pl.CostEstimate(
            flops=4 * 10**9, bytes_accessed=12 * 2**20, transcendentals=2 * 10**5
        ),
    )(place, table_of, *small, packed)


def pack_kernel(down, up, top1, top2, packed_hbm, packed, arrived):
    moves = [(down, 0)]
    moves += [(up.at[:, pl.ds(k * E, E)], WIDE + k * E) for k in range(TABLES + 1)]
    moves += [(top1.at[:, pl.ds(h * E, E)], (2 + h) * WIDE) for h in range(2)]
    moves += [(top2.at[:, pl.ds(h * E, E)], 4 * WIDE + h * TOP) for h in range(2)]
    copies = [
        pltpu.make_async_copy(source, packed.at[pl.ds(first, source.shape[0])], arrived.at[i])
        for i, (source, first) in enumerate(moves)
    ]
    for copy in copies:
        copy.start()
    for copy in copies:
        copy.wait()
    result = pltpu.make_async_copy(packed, packed_hbm, arrived.at[len(moves)])
    result.start()
    result.wait()


def pack(*weights):
    anywhere = pl.BlockSpec(memory_space=pl.ANY)
    return pl.pallas_call(
        pack_kernel,
        out_shape=jax.ShapeDtypeStruct((PACKED, E), BF),
        in_specs=[anywhere] * len(weights),
        out_specs=anywhere,
        scratch_shapes=[
            pltpu.VMEM((PACKED, E), BF),
            pltpu.SemaphoreType.DMA((TABLES + 7,)),
        ],
        compiler_params=pltpu.CompilerParams(vmem_limit_bytes=60 * 2**20),
        cost_estimate=pl.CostEstimate(flops=0, bytes_accessed=10 * 2**20, transcendentals=0),
    )(*weights)


def lanes_kernel(place, counts, out):
    my_yh = place[1]
    at = lax.broadcasted_iota(jnp.int32, (LOOK, LOOK), 0)
    to = lax.broadcasted_iota(jnp.int32, (LOOK, LOOK), 1)
    yh = (to // 4 % 2) * 2 + (my_yh + to // 8) % 2
    source = (to // 16 % X) * 32 + yh * 8 + (to // 64) * 4 + to % 4
    turned = (at == source).astype(BF)
    out[...] = dot(counts[...].astype(F32).astype(BF), turned).astype(BF)


def turn_lanes(place, counts):
    rows = counts.shape[0] // 8
    return pl.pallas_call(
        lanes_kernel,
        out_shape=jax.ShapeDtypeStruct(counts.shape, BF),
        grid=(8,),
        in_specs=[
            pl.BlockSpec(memory_space=pltpu.SMEM),
            pl.BlockSpec((rows, LOOK), lambda i: (i, 0)),
        ],
        out_specs=pl.BlockSpec((rows, LOOK), lambda i: (i, 0)),
        cost_estimate=pl.CostEstimate(
            flops=2 * 10**8, bytes_accessed=3 * 2**20, transcendentals=0
        ),
    )(place, counts)


def pair_kernel(_, halves, out):
    def one_block(i, carry):
        at = pl.ds(i * 256, 256)
        out[at] = (halves[0, at].astype(F32) + halves[1, at].astype(F32)).astype(BF)
        return carry

    lax.fori_loop(0, out.shape[0] // 256, one_block, 0, unroll=2)


def sum_kernel(place, parts, out):
    to = lax.broadcasted_iota(jnp.int32, (E, E), 0)
    at = lax.broadcasted_iota(jnp.int32, (E, E), 1)
    yh = to // 64
    turned = (
        at == (to // 4 % Z) * 16 + ((place[1] + yh) % 2) * 8 + (yh // 2) * 4 + to % 4
    ).astype(BF)
    total = parts[0].astype(F32)
    for i in range(1, parts.shape[0]):
        total = total + parts[i].astype(F32)
    out[...] = dot(turned, total.astype(BF)).astype(BF)


def fold(kernel, place, parts):
    return pl.pallas_call(
        kernel,
        out_shape=jax.ShapeDtypeStruct(parts.shape[1:], BF),
        in_specs=[
            pl.BlockSpec(memory_space=pltpu.SMEM),
            pl.BlockSpec(memory_space=pltpu.VMEM),
        ],
        out_specs=pl.BlockSpec(memory_space=pltpu.VMEM),
        compiler_params=pltpu.CompilerParams(vmem_limit_bytes=12 * 2**20),
        cost_estimate=pl.CostEstimate(
            flops=5 * 10**7, bytes_accessed=3 * 2**20, transcendentals=0
        ),
    )(place, parts)


def swap(value, axes):
    return lax.all_to_all(value, axes, split_axis=0, concat_axis=0, tiled=True)


def add_up(value):
    return jnp.sum(value.astype(F32), axis=0)


def turn(value, axis, size, shift):
    return lax.ppermute(value, axis, [(i, (i + shift) % size) for i in range(size)])


def shards(
    table,
    row_ids,
    pool_counts,
    table_of,
    dense_feat,
    labels,
    w_bottom1,
    w_bottom2,
    cross_down,
    cross_up,
    w_top1,
    w_top2,
    w_out,
):
    my_x, my_yh, my_c = lax.axis_index("x"), lax.axis_index("yh"), lax.axis_index("c")
    place = jnp.stack([my_x, my_yh, my_c]).astype(jnp.int32)
    first = my_x * 32 + jnp.bitwise_and(my_yh, 1) * 8 + my_c * 4
    span = lax.dynamic_slice(row_ids, (0, first), (1, 20))[0]
    ids = jnp.concatenate([span[:4], span[16:]])
    mine = jnp.take(table, ids, axis=0, mode="clip").astype(BF)
    mine = jnp.broadcast_to(mine, (SHARDS, 8, E))
    mine, pool_counts = lax.optimization_barrier((mine, pool_counts))
    looked = swap(mine, MP)
    counts = turn_lanes(place, pool_counts).reshape(SHARDS, N, LOOK)
    counts, *weights = lax.optimization_barrier((counts, cross_down, cross_up, w_top1, w_top2))
    packed = pack(*weights)
    looked, counts, packed = lax.optimization_barrier((looked, counts, packed))
    counts = swap(counts, MP)
    exchanged = lax.ppermute(looked, "yh", [(i, i ^ 1) for i in range(YH)])
    looked = jnp.concatenate([looked, exchanged], axis=1)
    looked = jnp.stack([looked] + [turn(looked, "x", X, k) for k in range(1, X)])
    others = turn(looked, "c", CORES, 1)

    hidden = lax.dot_general(
        dense_feat, w_bottom1, (((0,), (0,)), ((), ())), preferred_element_type=F32
    )
    hidden = jax.nn.relu(hidden).astype(BF)
    bottom = jax.nn.relu(dot(hidden, w_bottom2)).astype(BF)

    grads, logits = run_step(
        place,
        table_of,
        (bottom, labels.reshape(N, 1), w_out.reshape(1, -1), counts, looked, others),
        packed,
    )
    grads = swap(grads.reshape(CORES, X * YL * Z * 16, E), "c")
    grads = fold(pair_kernel, place, grads).reshape(X * YL, Z * 16, E)
    grads = fold(sum_kernel, place, swap(grads, ("x", "yl"))).reshape(YH * Z, 4, E)
    grads = add_up(swap(grads, ("yh", "z")))
    return grads, logits.reshape(N)


def solution(mesh):
    fine = Mesh(mesh.devices.reshape(X, YH, CORES, Z, YL), REP + MP)
    both = REP + MP
    return jax.shard_map(
        shards,
        mesh=fine,
        in_specs=(
            P(MP, None),
            P(MP, None),
            P(REP, MP),
            P(),
            P(None, both),
            P(both),
            P(),
            P(),
            P(),
            P(),
            P(),
            P(),
            P(),
        ),
        out_specs=(P(REP, MP), P(both)),
        check_vma=False,
    )
```

```python
import functools

import jax
import jax.numpy as jnp
from jax import lax
from jax.experimental import pallas as pl
from jax.experimental.pallas import tpu as pltpu
from jax.sharding import Mesh
from jax.sharding import PartitionSpec as P

X, YH, CORES, Z, YL = 4, 4, 2, 16, 2
REP = ("x", "yh", "c")
MP = ("z", "yl")
SHARDS = Z * YL
TABLES = 8
PER = SHARDS // TABLES
E = 256
N = 128
LOOK = 128
BF = jnp.bfloat16
F32 = jnp.float32


def silu_slope(value, sig):
    return sig + value * sig * (1.0 - sig)


def dot(a, b):
    return jnp.dot(a, b, preferred_element_type=F32)


def dot_nt(a, b):
    return lax.dot_general(a, b, (((1,), (1,)), ((), ())), preferred_element_type=F32)


def dot_tn(a, b):
    return lax.dot_general(a, b, (((0,), (0,)), ((), ())), preferred_element_type=F32)


def split_dot(value, weights):
    high = value.astype(BF)
    low = (value - high.astype(F32)).astype(BF)
    return dot(high, weights) + dot(low, weights)


def cols(k):
    return slice(k * E, (k + 1) * E)


WIDE = (TABLES + 1) * E
TOP = 512
PIECES = ((0, WIDE), (WIDE, WIDE), (2 * WIDE, 2 * WIDE), (4 * WIDE, 2 * TOP))
PACKED = 4 * WIDE + 2 * TOP


def step_kernel(
    place,
    table_of,
    bottom,
    labels,
    w_out,
    counts,
    own,
    other,
    packed_hbm,
    grads,
    logits_out,
    packed,
    feats,
    scaled,
    emb_grad,
    order,
    filled,
    arrived,
):
    copies = [
        pltpu.make_async_copy(
            packed_hbm.at[pl.ds(first, rows)], packed.at[pl.ds(first, rows)], arrived.at[i]
        )
        for i, (first, rows) in enumerate(PIECES)
    ]
    for copy in copies:
        copy.start()
    my_x, my_c = place[0], place[2]

    def down(k):
        return packed[cols(k), :]

    def up(k):
        return packed[cols(TABLES + 1 + k), :]

    def top1(k, half):
        return packed[cols((2 + half) * (TABLES + 1) + k), :]

    def top2(half):
        return packed[4 * WIDE + half * TOP : 4 * WIDE + (half + 1) * TOP, :]

    for t in range(TABLES):
        filled[t] = 0
    for m in range(SHARDS):
        t = table_of[m]
        k = filled[t]
        order[t * PER + k] = m
        filled[t] = k + 1

    feats[:, cols(0)] = bottom[...].astype(F32)
    for t in range(TABLES):
        acc = None
        for k in range(PER):
            m = order[t * PER + k]
            turns = [lax.rem(my_x + X - x, X) for x in range(X)]
            near = [own[k_x, m] for k_x in turns]
            far = [other[k_x, m] for k_x in turns]
            rows = jnp.concatenate(
                [jnp.where(my_c == 0, a, b) for a, b in zip(near, far)]
                + [jnp.where(my_c == 0, b, a) for a, b in zip(near, far)],
                axis=0,
            )
            term = dot(counts[m], rows)
            acc = term if acc is None else acc + term
        feats[:, cols(t + 1)] = acc

    copies[0].wait()
    low = split_dot(feats[...], packed[0:WIDE, :])
    low_high = low.astype(BF)
    low_rest = (low - low_high.astype(F32)).astype(BF)
    copies[1].wait()
    copies[2].wait()
    pre_one = [None, None]
    for k in range(TABLES + 1):
        scale = dot(low_high, up(k)) + dot(low_rest, up(k))
        scaled[:, cols(k)] = scale
        feat = feats[:, cols(k)]
        crossed = feat * scale + feat
        for half in range(2):
            term = split_dot(crossed, top1(k, half))
            pre_one[half] = term if k == 0 else pre_one[half] + term
    pre_one = jnp.concatenate(pre_one, axis=1)
    copies[3].wait()
    sig_one = jax.nn.sigmoid(pre_one)
    act_one = pre_one * sig_one
    pre_two = jnp.concatenate([split_dot(act_one, top2(0)), split_dot(act_one, top2(1))], axis=1)
    sig_two = jax.nn.sigmoid(pre_two)
    head = w_out[...]
    logits = jnp.sum(pre_two * sig_two * head, axis=1, keepdims=True)
    across = lax.broadcasted_iota(jnp.int32, (N, N), 0) == lax.broadcasted_iota(
        jnp.int32, (N, N), 1
    )
    logits_out[...] = jnp.sum(jnp.where(across, logits, 0.0), axis=0, keepdims=True)
    logit_grad = (jax.nn.sigmoid(logits) - labels[...].astype(F32)) * (1.0 / 32.0)
    grad_two = (logit_grad * head * silu_slope(pre_two, sig_two)).astype(BF)
    grad_act = dot_nt(grad_two[:, cols(0)], top2(0)) + dot_nt(grad_two[:, cols(1)], top2(1))
    grad_one = (grad_act * silu_slope(pre_one, sig_one)).astype(BF)
    low_grad = None
    for k in range(TABLES + 1):
        part = dot_nt(grad_one[:, cols(0)], top1(k, 0)) + dot_nt(grad_one[:, cols(1)], top1(k, 1))
        term = dot_nt((part * feats[:, cols(k)]).astype(BF), up(k))
        low_grad = term if low_grad is None else low_grad + term
        if k > 0:
            scaled[:, cols(k)] = part * (scaled[:, cols(k)] + 1.0)
    low_grad = low_grad.astype(BF)
    for t in range(TABLES):
        back = dot_nt(low_grad, down(t + 1))
        emb_grad[t] = (scaled[:, cols(t + 1)] + back).astype(BF)

    def one_shard(m, carry):
        terms = dot_tn(counts[m], emb_grad[table_of[m]]).astype(BF)
        for c in range(CORES):
            for x in range(X):
                at = (c * X + x) * 16
                grads[c, x, m % YL, m // YL] = terms[at : at + 16]
        return carry

    lax.fori_loop(0, SHARDS, one_shard, 0, unroll=8)


def run_step(place, table_of, small, packed):
    smem = pl.BlockSpec(memory_space=pltpu.SMEM)
    vmem = pl.BlockSpec(memory_space=pltpu.VMEM)
    hbm = pl.BlockSpec(memory_space=pl.ANY)
    return pl.pallas_call(
        step_kernel,
        out_shape=(
            jax.ShapeDtypeStruct((CORES, X, YL, Z, 16, E), BF),
            jax.ShapeDtypeStruct((1, N), F32),
        ),
        in_specs=[smem, smem] + [vmem] * len(small) + [hbm],
        out_specs=(vmem, vmem),
        scratch_shapes=[
            pltpu.VMEM((PACKED, E), BF),
            pltpu.VMEM((N, (TABLES + 1) * E), F32),
            pltpu.VMEM((N, (TABLES + 1) * E), F32),
            pltpu.VMEM((TABLES, N, E), BF),
            pltpu.SMEM((SHARDS,), jnp.int32),
            pltpu.SMEM((TABLES,), jnp.int32),
            pltpu.SemaphoreType.DMA((len(PIECES),)),
        ],
        compiler_params=pltpu.CompilerParams(vmem_limit_bytes=46 * 2**20),
        cost_estimate=pl.CostEstimate(
            flops=4 * 10**9, bytes_accessed=12 * 2**20, transcendentals=2 * 10**5
        ),
    )(place, table_of, *small, packed)


def pack_kernel(down, up, top1, top2, packed_hbm, packed, arrived):
    moves = [(down, 0)]
    moves += [(up.at[:, pl.ds(k * E, E)], WIDE + k * E) for k in range(TABLES + 1)]
    moves += [(top1.at[:, pl.ds(h * E, E)], (2 + h) * WIDE) for h in range(2)]
    moves += [(top2.at[:, pl.ds(h * E, E)], 4 * WIDE + h * TOP) for h in range(2)]
    copies = [
        pltpu.make_async_copy(source, packed.at[pl.ds(first, source.shape[0])], arrived.at[i])
        for i, (source, first) in enumerate(moves)
    ]
    for copy in copies:
        copy.start()
    for copy in copies:
        copy.wait()
    result = pltpu.make_async_copy(packed, packed_hbm, arrived.at[len(moves)])
    result.start()
    result.wait()


def pack(*weights):
    anywhere = pl.BlockSpec(memory_space=pl.ANY)
    return pl.pallas_call(
        pack_kernel,
        out_shape=jax.ShapeDtypeStruct((PACKED, E), BF),
        in_specs=[anywhere] * len(weights),
        out_specs=anywhere,
        scratch_shapes=[
            pltpu.VMEM((PACKED, E), BF),
            pltpu.SemaphoreType.DMA((TABLES + 7,)),
        ],
        compiler_params=pltpu.CompilerParams(vmem_limit_bytes=60 * 2**20),
        cost_estimate=pl.CostEstimate(flops=0, bytes_accessed=10 * 2**20, transcendentals=0),
    )(*weights)


def lanes_kernel(place, counts, out):
    my_yh = place[1]
    at = lax.broadcasted_iota(jnp.int32, (LOOK, LOOK), 0)
    to = lax.broadcasted_iota(jnp.int32, (LOOK, LOOK), 1)
    yh = (to // 4 % 2) * 2 + (my_yh + to // 8) % 2
    source = (to // 16 % X) * 32 + yh * 8 + (to // 64) * 4 + to % 4
    turned = (at == source).astype(BF)
    out[...] = dot(counts[...].astype(F32).astype(BF), turned).astype(BF)


def turn_lanes(place, counts):
    rows = counts.shape[0] // 2
    return pl.pallas_call(
        lanes_kernel,
        out_shape=jax.ShapeDtypeStruct(counts.shape, BF),
        grid=(2,),
        in_specs=[
            pl.BlockSpec(memory_space=pltpu.SMEM),
            pl.BlockSpec((rows, LOOK), lambda i: (i, 0)),
        ],
        out_specs=pl.BlockSpec((rows, LOOK), lambda i: (i, 0)),
        compiler_params=pltpu.CompilerParams(vmem_limit_bytes=60 * 2**20),
        cost_estimate=pl.CostEstimate(
            flops=2 * 10**8, bytes_accessed=3 * 2**20, transcendentals=0
        ),
    )(place, counts)


def pair_kernel(_, halves, out):
    def one_block(i, carry):
        at = pl.ds(i * 256, 256)
        out[at] = (halves[0, at].astype(F32) + halves[1, at].astype(F32)).astype(BF)
        return carry

    lax.fori_loop(0, out.shape[0] // 256, one_block, 0, unroll=2)


def sum_kernel(place, parts, out):
    to = lax.broadcasted_iota(jnp.int32, (E, E), 0)
    at = lax.broadcasted_iota(jnp.int32, (E, E), 1)
    yh = to // 64
    turned = (
        at == (to // 4 % Z) * 16 + ((place[1] + yh) % 2) * 8 + (yh // 2) * 4 + to % 4
    ).astype(BF)
    total = parts[0].astype(F32)
    for i in range(1, parts.shape[0]):
        total = total + parts[i].astype(F32)
    out[...] = dot(turned, total.astype(BF)).astype(BF)


def fold(kernel, place, parts):
    return pl.pallas_call(
        kernel,
        out_shape=jax.ShapeDtypeStruct(parts.shape[1:], BF),
        in_specs=[
            pl.BlockSpec(memory_space=pltpu.SMEM),
            pl.BlockSpec(memory_space=pltpu.VMEM),
        ],
        out_specs=pl.BlockSpec(memory_space=pltpu.VMEM),
        compiler_params=pltpu.CompilerParams(vmem_limit_bytes=12 * 2**20),
        cost_estimate=pl.CostEstimate(
            flops=5 * 10**7, bytes_accessed=3 * 2**20, transcendentals=0
        ),
    )(place, parts)


def swap(value, axes):
    return lax.all_to_all(value, axes, split_axis=0, concat_axis=0, tiled=True)


def add_up(value):
    return jnp.sum(value.astype(F32), axis=0)


def turn(value, axis, size, shift):
    return lax.ppermute(value, axis, [(i, (i + shift) % size) for i in range(size)])


def shards(
    table,
    row_ids,
    pool_counts,
    table_of,
    dense_feat,
    labels,
    w_bottom1,
    w_bottom2,
    cross_down,
    cross_up,
    w_top1,
    w_top2,
    w_out,
):
    my_x, my_yh, my_c = lax.axis_index("x"), lax.axis_index("yh"), lax.axis_index("c")
    place = jnp.stack([my_x, my_yh, my_c]).astype(jnp.int32)
    first = my_x * 32 + jnp.bitwise_and(my_yh, 1) * 8 + my_c * 4
    span = lax.dynamic_slice(row_ids, (0, first), (1, 20))[0]
    ids = jnp.concatenate([span[:4], span[16:]])
    mine = jnp.take(table, ids, axis=0, mode="clip").astype(BF)
    mine = jnp.broadcast_to(mine, (SHARDS, 8, E))
    mine, pool_counts = lax.optimization_barrier((mine, pool_counts))
    looked = swap(mine, MP)
    counts = turn_lanes(place, pool_counts).reshape(SHARDS, N, LOOK)
    looked, counts = lax.optimization_barrier((looked, counts))
    counts = swap(counts, MP)
    exchanged = lax.ppermute(looked, "yh", [(i, i ^ 1) for i in range(YH)])
    looked = jnp.concatenate([looked, exchanged], axis=1)
    looked, *weights = lax.optimization_barrier((looked, cross_down, cross_up, w_top1, w_top2))
    packed = pack(*weights)
    looked = jnp.stack([looked] + [turn(looked, "x", X, k) for k in range(1, X)])
    others = turn(looked, "c", CORES, 1)

    hidden = lax.dot_general(
        dense_feat, w_bottom1, (((0,), (0,)), ((), ())), preferred_element_type=F32
    )
    hidden = jax.nn.relu(hidden).astype(BF)
    bottom = jax.nn.relu(dot(hidden, w_bottom2)).astype(BF)

    grads, logits = run_step(
        place,
        table_of,
        (bottom, labels.reshape(N, 1), w_out.reshape(1, -1), counts, looked, others),
        packed,
    )
    grads = swap(grads.reshape(CORES, X * YL * Z * 16, E), "c")
    grads = fold(pair_kernel, place, grads).reshape(X * YL, Z * 16, E)
    grads = fold(sum_kernel, place, swap(grads, ("x", "yl"))).reshape(YH * Z, 4, E)
    grads = add_up(swap(grads, ("yh", "z")))
    return grads, logits.reshape(N)


def solution(mesh):
    fine = Mesh(mesh.devices.reshape(X, YH, CORES, Z, YL), REP + MP)
    both = REP + MP
    return jax.shard_map(
        shards,
        mesh=fine,
        in_specs=(
            P(MP, None),
            P(MP, None),
            P(REP, MP),
            P(),
            P(None, both),
            P(both),
            P(),
            P(),
            P(),
            P(),
            P(),
            P(),
            P(),
        ),
        out_specs=(P(REP, MP), P(both)),
        check_vma=False,
    )
```

```python
import functools

import jax
import jax.numpy as jnp
from jax import lax
from jax.experimental import pallas as pl
from jax.experimental.pallas import tpu as pltpu
from jax.sharding import Mesh
from jax.sharding import PartitionSpec as P

X, YH, CORES, Z, YL = 4, 4, 2, 16, 2
REP = ("x", "yh", "c")
MP = ("z", "yl")
SHARDS = Z * YL
TABLES = 8
PER = SHARDS // TABLES
E = 256
N = 128
LOOK = 128
BF = jnp.bfloat16
F32 = jnp.float32


def silu_slope(value, sig):
    return sig + value * sig * (1.0 - sig)


def dot(a, b):
    return jnp.dot(a, b, preferred_element_type=F32)


def dot_nt(a, b):
    return lax.dot_general(a, b, (((1,), (1,)), ((), ())), preferred_element_type=F32)


def dot_tn(a, b):
    return lax.dot_general(a, b, (((0,), (0,)), ((), ())), preferred_element_type=F32)


def split_dot(value, weights):
    high = value.astype(BF)
    low = (value - high.astype(F32)).astype(BF)
    return dot(high, weights) + dot(low, weights)


def cols(k):
    return slice(k * E, (k + 1) * E)


WIDE = (TABLES + 1) * E
TOP = 512
PIECES = ((0, WIDE), (WIDE, WIDE), (2 * WIDE, 2 * WIDE), (4 * WIDE, 2 * TOP))
PACKED = 4 * WIDE + 2 * TOP


def step_kernel(
    place,
    table_of,
    bottom,
    labels,
    w_out,
    counts,
    own,
    other,
    packed_hbm,
    grads,
    logits_out,
    packed,
    feats,
    scaled,
    emb_grad,
    order,
    filled,
    arrived,
):
    copies = [
        pltpu.make_async_copy(
            packed_hbm.at[pl.ds(first, rows)], packed.at[pl.ds(first, rows)], arrived.at[i]
        )
        for i, (first, rows) in enumerate(PIECES)
    ]
    for copy in copies:
        copy.start()
    my_x, my_c, my_yl = place[0], place[2], place[3]

    def down(k):
        return packed[cols(k), :]

    def up(k):
        return packed[cols(TABLES + 1 + k), :]

    def top1(k, half):
        return packed[cols((2 + half) * (TABLES + 1) + k), :]

    def top2(half):
        return packed[4 * WIDE + half * TOP : 4 * WIDE + (half + 1) * TOP, :]

    for t in range(TABLES):
        filled[t] = 0
    for m in range(SHARDS):
        t = table_of[m]
        k = filled[t]
        order[t * PER + k] = m
        filled[t] = k + 1

    feats[:, cols(0)] = bottom[...].astype(F32)
    for t in range(TABLES):
        acc = None
        for k in range(PER):
            m = order[t * PER + k]
            turns = [lax.rem(my_x + X - x, X) for x in range(X)]
            at = lax.bitwise_xor(m, my_yl)
            near = [own[k_x, at] for k_x in turns]
            far = [other[k_x, at] for k_x in turns]
            rows = jnp.concatenate(
                [jnp.where(my_c == 0, a, b) for a, b in zip(near, far)]
                + [jnp.where(my_c == 0, b, a) for a, b in zip(near, far)],
                axis=0,
            )
            term = dot(counts[m], rows)
            acc = term if acc is None else acc + term
        feats[:, cols(t + 1)] = acc

    copies[0].wait()
    low = split_dot(feats[...], packed[0:WIDE, :])
    low_high = low.astype(BF)
    low_rest = (low - low_high.astype(F32)).astype(BF)
    copies[1].wait()
    copies[2].wait()
    pre_one = [None, None]
    for k in range(TABLES + 1):
        scale = dot(low_high, up(k)) + dot(low_rest, up(k))
        scaled[:, cols(k)] = scale
        feat = feats[:, cols(k)]
        crossed = feat * scale + feat
        for half in range(2):
            term = split_dot(crossed, top1(k, half))
            pre_one[half] = term if k == 0 else pre_one[half] + term
    pre_one = jnp.concatenate(pre_one, axis=1)
    copies[3].wait()
    sig_one = jax.nn.sigmoid(pre_one)
    act_one = pre_one * sig_one
    pre_two = jnp.concatenate([split_dot(act_one, top2(0)), split_dot(act_one, top2(1))], axis=1)
    sig_two = jax.nn.sigmoid(pre_two)
    head = w_out[...]
    logits = jnp.sum(pre_two * sig_two * head, axis=1, keepdims=True)
    across = lax.broadcasted_iota(jnp.int32, (N, N), 0) == lax.broadcasted_iota(
        jnp.int32, (N, N), 1
    )
    logits_out[...] = jnp.sum(jnp.where(across, logits, 0.0), axis=0, keepdims=True)
    logit_grad = (jax.nn.sigmoid(logits) - labels[...].astype(F32)) * (1.0 / 32.0)
    grad_two = (logit_grad * head * silu_slope(pre_two, sig_two)).astype(BF)
    grad_act = dot_nt(grad_two[:, cols(0)], top2(0)) + dot_nt(grad_two[:, cols(1)], top2(1))
    grad_one = (grad_act * silu_slope(pre_one, sig_one)).astype(BF)
    low_grad = None
    for k in range(TABLES + 1):
        part = dot_nt(grad_one[:, cols(0)], top1(k, 0)) + dot_nt(grad_one[:, cols(1)], top1(k, 1))
        term = dot_nt((part * feats[:, cols(k)]).astype(BF), up(k))
        low_grad = term if low_grad is None else low_grad + term
        if k > 0:
            scaled[:, cols(k)] = part * (scaled[:, cols(k)] + 1.0)
    low_grad = low_grad.astype(BF)
    for t in range(TABLES):
        back = dot_nt(low_grad, down(t + 1))
        emb_grad[t] = (scaled[:, cols(t + 1)] + back).astype(BF)

    def one_shard(m, carry):
        terms = dot_tn(counts[m], emb_grad[table_of[m]]).astype(BF)
        for c in range(CORES):
            for x in range(X):
                at = (c * X + x) * 16
                grads[c, x, m % YL, m // YL] = terms[at : at + 16]
        return carry

    lax.fori_loop(0, SHARDS, one_shard, 0, unroll=8)


def run_step(place, table_of, small, packed):
    smem = pl.BlockSpec(memory_space=pltpu.SMEM)
    vmem = pl.BlockSpec(memory_space=pltpu.VMEM)
    hbm = pl.BlockSpec(memory_space=pl.ANY)
    return pl.pallas_call(
        step_kernel,
        out_shape=(
            jax.ShapeDtypeStruct((CORES, X, YL, Z, 16, E), BF),
            jax.ShapeDtypeStruct((1, N), F32),
        ),
        in_specs=[smem, smem] + [vmem] * len(small) + [hbm],
        out_specs=(vmem, vmem),
        scratch_shapes=[
            pltpu.VMEM((PACKED, E), BF),
            pltpu.VMEM((N, (TABLES + 1) * E), F32),
            pltpu.VMEM((N, (TABLES + 1) * E), F32),
            pltpu.VMEM((TABLES, N, E), BF),
            pltpu.SMEM((SHARDS,), jnp.int32),
            pltpu.SMEM((TABLES,), jnp.int32),
            pltpu.SemaphoreType.DMA((len(PIECES),)),
        ],
        compiler_params=pltpu.CompilerParams(vmem_limit_bytes=46 * 2**20),
        cost_estimate=pl.CostEstimate(
            flops=4 * 10**9, bytes_accessed=12 * 2**20, transcendentals=2 * 10**5
        ),
    )(place, table_of, *small, packed)


def pack_kernel(down, up, top1, top2, packed_hbm, packed, arrived):
    moves = [(down, 0)]
    moves += [(up.at[:, pl.ds(k * E, E)], WIDE + k * E) for k in range(TABLES + 1)]
    moves += [(top1.at[:, pl.ds(h * E, E)], (2 + h) * WIDE) for h in range(2)]
    moves += [(top2.at[:, pl.ds(h * E, E)], 4 * WIDE + h * TOP) for h in range(2)]
    copies = [
        pltpu.make_async_copy(source, packed.at[pl.ds(first, source.shape[0])], arrived.at[i])
        for i, (source, first) in enumerate(moves)
    ]
    for copy in copies:
        copy.start()
    for copy in copies:
        copy.wait()
    result = pltpu.make_async_copy(packed, packed_hbm, arrived.at[len(moves)])
    result.start()
    result.wait()


def pack(*weights):
    anywhere = pl.BlockSpec(memory_space=pl.ANY)
    return pl.pallas_call(
        pack_kernel,
        out_shape=jax.ShapeDtypeStruct((PACKED, E), BF),
        in_specs=[anywhere] * len(weights),
        out_specs=anywhere,
        scratch_shapes=[
            pltpu.VMEM((PACKED, E), BF),
            pltpu.SemaphoreType.DMA((TABLES + 7,)),
        ],
        compiler_params=pltpu.CompilerParams(vmem_limit_bytes=60 * 2**20),
        cost_estimate=pl.CostEstimate(flops=0, bytes_accessed=10 * 2**20, transcendentals=0),
    )(*weights)


def lanes_kernel(place, counts, out):
    my_yh = place[1]
    at = lax.broadcasted_iota(jnp.int32, (LOOK, LOOK), 0)
    to = lax.broadcasted_iota(jnp.int32, (LOOK, LOOK), 1)
    yh = (to // 4 % 2) * 2 + (my_yh + to // 8) % 2
    source = (to // 16 % X) * 32 + yh * 8 + (to // 64) * 4 + to % 4
    turned = (at == source).astype(BF)
    out[...] = dot(counts[...].astype(F32).astype(BF), turned).astype(BF)


def turn_lanes(place, counts):
    rows = counts.shape[0] // 2
    return pl.pallas_call(
        lanes_kernel,
        out_shape=jax.ShapeDtypeStruct(counts.shape, BF),
        grid=(2,),
        in_specs=[
            pl.BlockSpec(memory_space=pltpu.SMEM),
            pl.BlockSpec((rows, LOOK), lambda i: (i, 0)),
        ],
        out_specs=pl.BlockSpec((rows, LOOK), lambda i: (i, 0)),
        compiler_params=pltpu.CompilerParams(vmem_limit_bytes=60 * 2**20),
        cost_estimate=pl.CostEstimate(
            flops=2 * 10**8, bytes_accessed=3 * 2**20, transcendentals=0
        ),
    )(place, counts)


def pair_kernel(_, halves, out):
    def one_block(i, carry):
        at = pl.ds(i * 256, 256)
        out[at] = (halves[0, at].astype(F32) + halves[1, at].astype(F32)).astype(BF)
        return carry

    lax.fori_loop(0, out.shape[0] // 256, one_block, 0, unroll=2)


def sum_kernel(place, parts, out):
    to = lax.broadcasted_iota(jnp.int32, (E, E), 0)
    at = lax.broadcasted_iota(jnp.int32, (E, E), 1)
    yh = to // 64
    turned = (
        at == (to // 4 % Z) * 16 + ((place[1] + yh) % 2) * 8 + (yh // 2) * 4 + to % 4
    ).astype(BF)
    total = parts[0].astype(F32)
    for i in range(1, parts.shape[0]):
        total = total + parts[i].astype(F32)
    out[...] = dot(turned, total.astype(BF)).astype(BF)


def fold(kernel, place, parts):
    return pl.pallas_call(
        kernel,
        out_shape=jax.ShapeDtypeStruct(parts.shape[1:], BF),
        in_specs=[
            pl.BlockSpec(memory_space=pltpu.SMEM),
            pl.BlockSpec(memory_space=pltpu.VMEM),
        ],
        out_specs=pl.BlockSpec(memory_space=pltpu.VMEM),
        compiler_params=pltpu.CompilerParams(vmem_limit_bytes=12 * 2**20),
        cost_estimate=pl.CostEstimate(
            flops=5 * 10**7, bytes_accessed=3 * 2**20, transcendentals=0
        ),
    )(place, parts)


def swap(value, axes):
    return lax.all_to_all(value, axes, split_axis=0, concat_axis=0, tiled=True)


def add_up(value):
    return jnp.sum(value.astype(F32), axis=0)


def turn(value, axis, size, shift):
    return lax.ppermute(value, axis, [(i, (i + shift) % size) for i in range(size)])


def shards(
    table,
    row_ids,
    pool_counts,
    table_of,
    dense_feat,
    labels,
    w_bottom1,
    w_bottom2,
    cross_down,
    cross_up,
    w_top1,
    w_top2,
    w_out,
):
    my_x, my_yh, my_c = lax.axis_index("x"), lax.axis_index("yh"), lax.axis_index("c")
    place = jnp.stack([my_x, my_yh, my_c, lax.axis_index("yl")]).astype(jnp.int32)
    first = my_x * 32 + jnp.bitwise_and(my_yh, 1) * 8 + my_c * 4
    span = lax.dynamic_slice(row_ids, (0, first), (1, 20))[0]
    ids = jnp.concatenate([span[:4], span[16:]])
    mine = jnp.take(table, ids, axis=0, mode="clip").astype(BF)
    mine = jnp.broadcast_to(mine, (Z, 8, E))
    mine, pool_counts = lax.optimization_barrier((mine, pool_counts))
    looked = swap(mine, "z")
    counts = turn_lanes(place, pool_counts).reshape(SHARDS, N, LOOK)
    looked, counts = lax.optimization_barrier((looked, counts))
    counts = swap(counts, MP)
    looked = jnp.stack([looked, turn(looked, "yl", YL, 1)], axis=1).reshape(SHARDS, 8, E)
    exchanged = lax.ppermute(looked, "yh", [(i, i ^ 1) for i in range(YH)])
    looked = jnp.concatenate([looked, exchanged], axis=1)
    looked, *weights = lax.optimization_barrier((looked, cross_down, cross_up, w_top1, w_top2))
    packed = pack(*weights)
    looked = jnp.stack([looked] + [turn(looked, "x", X, k) for k in range(1, X)])
    others = turn(looked, "c", CORES, 1)

    hidden = lax.dot_general(
        dense_feat, w_bottom1, (((0,), (0,)), ((), ())), preferred_element_type=F32
    )
    hidden = jax.nn.relu(hidden).astype(BF)
    bottom = jax.nn.relu(dot(hidden, w_bottom2)).astype(BF)

    grads, logits = run_step(
        place,
        table_of,
        (bottom, labels.reshape(N, 1), w_out.reshape(1, -1), counts, looked, others),
        packed,
    )
    grads = swap(grads.reshape(CORES, X * YL * Z * 16, E), "c")
    grads = fold(pair_kernel, place, grads).reshape(X * YL, Z * 16, E)
    grads = fold(sum_kernel, place, swap(grads, ("x", "yl"))).reshape(YH * Z, 4, E)
    grads = add_up(swap(grads, ("yh", "z")))
    return grads, logits.reshape(N)


def solution(mesh):
    fine = Mesh(mesh.devices.reshape(X, YH, CORES, Z, YL), REP + MP)
    both = REP + MP
    return jax.shard_map(
        shards,
        mesh=fine,
        in_specs=(
            P(MP, None),
            P(MP, None),
            P(REP, MP),
            P(),
            P(None, both),
            P(both),
            P(),
            P(),
            P(),
            P(),
            P(),
            P(),
            P(),
        ),
        out_specs=(P(REP, MP), P(both)),
        check_vma=False,
    )
```

```python
import functools

import jax
import jax.numpy as jnp
from jax import lax
from jax.experimental import pallas as pl
from jax.experimental.pallas import tpu as pltpu
from jax.sharding import Mesh
from jax.sharding import PartitionSpec as P

X, YH, CORES, Z, YL = 4, 4, 2, 16, 2
REP = ("x", "yh", "c")
MP = ("z", "yl")
SHARDS = Z * YL
TABLES = 8
PER = SHARDS // TABLES
E = 256
N = 128
LOOK = 128
BF = jnp.bfloat16
F32 = jnp.float32


def silu_slope(value, sig):
    return sig + value * sig * (1.0 - sig)


def dot(a, b):
    return jnp.dot(a, b, preferred_element_type=F32)


def dot_nt(a, b):
    return lax.dot_general(a, b, (((1,), (1,)), ((), ())), preferred_element_type=F32)


def dot_tn(a, b):
    return lax.dot_general(a, b, (((0,), (0,)), ((), ())), preferred_element_type=F32)


def split_dot(value, weights):
    high = value.astype(BF)
    low = (value - high.astype(F32)).astype(BF)
    return dot(high, weights) + dot(low, weights)


def cols(k):
    return slice(k * E, (k + 1) * E)


WIDE = (TABLES + 1) * E
TOP = 512
PIECES = ((0, WIDE), (WIDE, WIDE), (2 * WIDE, 2 * WIDE), (4 * WIDE, 2 * TOP))
PACKED = 4 * WIDE + 2 * TOP


def step_kernel(
    place,
    table_of,
    bottom,
    labels,
    w_out,
    counts,
    own,
    other,
    packed_hbm,
    grads,
    logits_out,
    packed,
    feats,
    scaled,
    emb_grad,
    order,
    filled,
    arrived,
):
    copies = [
        pltpu.make_async_copy(
            packed_hbm.at[pl.ds(first, rows)], packed.at[pl.ds(first, rows)], arrived.at[i]
        )
        for i, (first, rows) in enumerate(PIECES)
    ]
    for copy in copies:
        copy.start()
    my_x, my_c, my_yl = place[0], place[2], place[3]

    def down(k):
        return packed[cols(k), :]

    def up(k):
        return packed[cols(TABLES + 1 + k), :]

    def top1(k, half):
        return packed[cols((2 + half) * (TABLES + 1) + k), :]

    def top2(half):
        return packed[4 * WIDE + half * TOP : 4 * WIDE + (half + 1) * TOP, :]

    for t in range(TABLES):
        filled[t] = 0
    for m in range(SHARDS):
        t = table_of[m]
        k = filled[t]
        order[t * PER + k] = m
        filled[t] = k + 1

    feats[:, cols(0)] = bottom[...].astype(F32)
    for t in range(TABLES):
        acc = None
        for k in range(PER):
            m = order[t * PER + k]
            turns = [lax.rem(my_x + X - x, X) for x in range(X)]
            at = lax.bitwise_xor(m, my_yl)
            near = [own[k_x, at] for k_x in turns]
            far = [other[k_x, at] for k_x in turns]
            rows = jnp.concatenate(
                [jnp.where(my_c == 0, a, b) for a, b in zip(near, far)]
                + [jnp.where(my_c == 0, b, a) for a, b in zip(near, far)],
                axis=0,
            )
            term = dot(counts[m], rows)
            acc = term if acc is None else acc + term
        feats[:, cols(t + 1)] = acc

    copies[0].wait()
    low = split_dot(feats[...], packed[0:WIDE, :])
    low_high = low.astype(BF)
    low_rest = (low - low_high.astype(F32)).astype(BF)
    copies[1].wait()
    copies[2].wait()
    pre_one = [None, None]
    for k in range(TABLES + 1):
        scale = dot(low_high, up(k)) + dot(low_rest, up(k))
        scaled[:, cols(k)] = scale
        feat = feats[:, cols(k)]
        crossed = feat * scale + feat
        for half in range(2):
            term = split_dot(crossed, top1(k, half))
            pre_one[half] = term if k == 0 else pre_one[half] + term
    pre_one = jnp.concatenate(pre_one, axis=1)
    copies[3].wait()
    sig_one = jax.nn.sigmoid(pre_one)
    act_one = pre_one * sig_one
    pre_two = jnp.concatenate([split_dot(act_one, top2(0)), split_dot(act_one, top2(1))], axis=1)
    sig_two = jax.nn.sigmoid(pre_two)
    head = w_out[...]
    logits = jnp.sum(pre_two * sig_two * head, axis=1, keepdims=True)
    across = lax.broadcasted_iota(jnp.int32, (N, N), 0) == lax.broadcasted_iota(
        jnp.int32, (N, N), 1
    )
    logits_out[...] = jnp.sum(jnp.where(across, logits, 0.0), axis=0, keepdims=True)
    logit_grad = (jax.nn.sigmoid(logits) - labels[...].astype(F32)) * (1.0 / 32.0)
    grad_two = (logit_grad * head * silu_slope(pre_two, sig_two)).astype(BF)
    grad_act = dot_nt(grad_two[:, cols(0)], top2(0)) + dot_nt(grad_two[:, cols(1)], top2(1))
    grad_one = (grad_act * silu_slope(pre_one, sig_one)).astype(BF)
    low_grad = None
    for k in range(TABLES + 1):
        part = dot_nt(grad_one[:, cols(0)], top1(k, 0)) + dot_nt(grad_one[:, cols(1)], top1(k, 1))
        term = dot_nt((part * feats[:, cols(k)]).astype(BF), up(k))
        low_grad = term if low_grad is None else low_grad + term
        if k > 0:
            scaled[:, cols(k)] = part * (scaled[:, cols(k)] + 1.0)
    low_grad = low_grad.astype(BF)
    for t in range(TABLES):
        back = dot_nt(low_grad, down(t + 1))
        emb_grad[t] = (scaled[:, cols(t + 1)] + back).astype(BF)

    def one_shard(m, carry):
        terms = dot_tn(counts[m], emb_grad[table_of[m]]).astype(BF)
        for c in range(CORES):
            for x in range(X):
                at = (c * X + x) * 16
                grads[c, x, m % YL, m // YL] = terms[at : at + 16]
        return carry

    lax.fori_loop(0, SHARDS, one_shard, 0, unroll=32)


def run_step(place, table_of, small, packed):
    smem = pl.BlockSpec(memory_space=pltpu.SMEM)
    vmem = pl.BlockSpec(memory_space=pltpu.VMEM)
    hbm = pl.BlockSpec(memory_space=pl.ANY)
    return pl.pallas_call(
        step_kernel,
        out_shape=(
            jax.ShapeDtypeStruct((CORES, X, YL, Z, 16, E), BF),
            jax.ShapeDtypeStruct((1, N), F32),
        ),
        in_specs=[smem, smem] + [vmem] * len(small) + [hbm],
        out_specs=(vmem, vmem),
        scratch_shapes=[
            pltpu.VMEM((PACKED, E), BF),
            pltpu.VMEM((N, (TABLES + 1) * E), F32),
            pltpu.VMEM((N, (TABLES + 1) * E), F32),
            pltpu.VMEM((TABLES, N, E), BF),
            pltpu.SMEM((SHARDS,), jnp.int32),
            pltpu.SMEM((TABLES,), jnp.int32),
            pltpu.SemaphoreType.DMA((len(PIECES),)),
        ],
        compiler_params=pltpu.CompilerParams(vmem_limit_bytes=46 * 2**20),
        cost_estimate=pl.CostEstimate(
            flops=4 * 10**9, bytes_accessed=12 * 2**20, transcendentals=2 * 10**5
        ),
    )(place, table_of, *small, packed)


def pack_kernel(down, up, top1, top2, packed_hbm, packed, arrived):
    moves = [(down, 0)]
    moves += [(up.at[:, pl.ds(k * E, E)], WIDE + k * E) for k in range(TABLES + 1)]
    moves += [(top1.at[:, pl.ds(h * E, E)], (2 + h) * WIDE) for h in range(2)]
    moves += [(top2.at[:, pl.ds(h * E, E)], 4 * WIDE + h * TOP) for h in range(2)]
    copies = [
        pltpu.make_async_copy(source, packed.at[pl.ds(first, source.shape[0])], arrived.at[i])
        for i, (source, first) in enumerate(moves)
    ]
    for copy in copies:
        copy.start()
    for copy in copies:
        copy.wait()
    result = pltpu.make_async_copy(packed, packed_hbm, arrived.at[len(moves)])
    result.start()
    result.wait()


def pack(*weights):
    anywhere = pl.BlockSpec(memory_space=pl.ANY)
    return pl.pallas_call(
        pack_kernel,
        out_shape=jax.ShapeDtypeStruct((PACKED, E), BF),
        in_specs=[anywhere] * len(weights),
        out_specs=anywhere,
        scratch_shapes=[
            pltpu.VMEM((PACKED, E), BF),
            pltpu.SemaphoreType.DMA((TABLES + 7,)),
        ],
        compiler_params=pltpu.CompilerParams(vmem_limit_bytes=60 * 2**20),
        cost_estimate=pl.CostEstimate(flops=0, bytes_accessed=10 * 2**20, transcendentals=0),
    )(*weights)


def lanes_kernel(place, counts, out):
    my_yh = place[1]
    at = lax.broadcasted_iota(jnp.int32, (LOOK, LOOK), 0)
    to = lax.broadcasted_iota(jnp.int32, (LOOK, LOOK), 1)
    yh = (to // 4 % 2) * 2 + (my_yh + to // 8) % 2
    source = (to // 16 % X) * 32 + yh * 8 + (to // 64) * 4 + to % 4
    turned = (at == source).astype(BF)
    out[...] = dot(counts[...].astype(F32).astype(BF), turned).astype(BF)


def turn_lanes(place, counts):
    rows = counts.shape[0] // 2
    return pl.pallas_call(
        lanes_kernel,
        out_shape=jax.ShapeDtypeStruct(counts.shape, BF),
        grid=(2,),
        in_specs=[
            pl.BlockSpec(memory_space=pltpu.SMEM),
            pl.BlockSpec((rows, LOOK), lambda i: (i, 0)),
        ],
        out_specs=pl.BlockSpec((rows, LOOK), lambda i: (i, 0)),
        compiler_params=pltpu.CompilerParams(vmem_limit_bytes=60 * 2**20),
        cost_estimate=pl.CostEstimate(
            flops=2 * 10**8, bytes_accessed=3 * 2**20, transcendentals=0
        ),
    )(place, counts)


def pair_kernel(_, halves, out):
    def one_block(i, carry):
        at = pl.ds(i * 256, 256)
        out[at] = (halves[0, at].astype(F32) + halves[1, at].astype(F32)).astype(BF)
        return carry

    lax.fori_loop(0, out.shape[0] // 256, one_block, 0, unroll=2)


def sum_kernel(place, parts, out):
    to = lax.broadcasted_iota(jnp.int32, (2 * E, E), 0)
    at = lax.broadcasted_iota(jnp.int32, (2 * E, E), 1)
    half, row = to % 2, to // 2
    yh = row // 64
    source = (row // 4 % Z) * 16 + ((place[1] + yh) % 2) * 8 + (yh // 2) * 4 + row % 4
    total = parts[0].astype(F32)
    for i in range(1, parts.shape[0]):
        total = total + parts[i].astype(F32)
    total = total.astype(BF)
    left = dot(((at == source) & (half == 0)).astype(BF), total[:, :LOOK])
    right = dot(((at == source) & (half == 1)).astype(BF), total[:, LOOK:])
    out[...] = (left + right).astype(BF)


def fold(kernel, place, parts, shape):
    return pl.pallas_call(
        kernel,
        out_shape=jax.ShapeDtypeStruct(shape, BF),
        in_specs=[
            pl.BlockSpec(memory_space=pltpu.SMEM),
            pl.BlockSpec(memory_space=pltpu.VMEM),
        ],
        out_specs=pl.BlockSpec(memory_space=pltpu.VMEM),
        compiler_params=pltpu.CompilerParams(vmem_limit_bytes=12 * 2**20),
        cost_estimate=pl.CostEstimate(
            flops=5 * 10**7, bytes_accessed=3 * 2**20, transcendentals=0
        ),
    )(place, parts)


def swap(value, axes):
    return lax.all_to_all(value, axes, split_axis=0, concat_axis=0, tiled=True)


def add_up(value):
    return jnp.sum(value.astype(F32), axis=0)


def turn(value, axis, size, shift):
    return lax.ppermute(value, axis, [(i, (i + shift) % size) for i in range(size)])


def shards(
    table,
    row_ids,
    pool_counts,
    table_of,
    dense_feat,
    labels,
    w_bottom1,
    w_bottom2,
    cross_down,
    cross_up,
    w_top1,
    w_top2,
    w_out,
):
    my_x, my_yh, my_c = lax.axis_index("x"), lax.axis_index("yh"), lax.axis_index("c")
    place = jnp.stack([my_x, my_yh, my_c, lax.axis_index("yl")]).astype(jnp.int32)
    first = my_x * 32 + jnp.bitwise_and(my_yh, 1) * 8 + my_c * 4
    span = lax.dynamic_slice(row_ids, (0, first), (1, 20))[0]
    ids = jnp.concatenate([span[:4], span[16:]])
    mine = jnp.take(table, ids, axis=0, mode="clip").astype(BF)
    mine = jnp.broadcast_to(mine, (Z, 8, E))
    mine, pool_counts = lax.optimization_barrier((mine, pool_counts))
    looked = swap(mine, "z")
    counts = turn_lanes(place, pool_counts).reshape(SHARDS, N, LOOK)
    looked, counts = lax.optimization_barrier((looked, counts))
    counts = swap(counts, MP)
    looked = jnp.stack([looked, turn(looked, "yl", YL, 1)], axis=1).reshape(SHARDS, 8, E)
    exchanged = lax.ppermute(looked, "yh", [(i, i ^ 1) for i in range(YH)])
    looked = jnp.concatenate([looked, exchanged], axis=1)
    looked, *weights = lax.optimization_barrier((looked, cross_down, cross_up, w_top1, w_top2))
    packed = pack(*weights)
    looked = jnp.stack([looked] + [turn(looked, "x", X, k) for k in range(1, X)])
    others = turn(looked, "c", CORES, 1)

    hidden = lax.dot_general(
        dense_feat, w_bottom1, (((0,), (0,)), ((), ())), preferred_element_type=F32
    )
    hidden = jax.nn.relu(hidden).astype(BF)
    bottom = jax.nn.relu(dot(hidden, w_bottom2)).astype(BF)

    grads, logits = run_step(
        place,
        table_of,
        (bottom, labels.reshape(N, 1), w_out.reshape(1, -1), counts, looked, others),
        packed,
    )
    grads = swap(grads.reshape(CORES, X * YL * Z * 16, E), "c")
    grads = fold(pair_kernel, place, grads, grads.shape[1:]).reshape(X * YL, Z * 16, E)
    grads = fold(sum_kernel, place, swap(grads, ("x", "yl")), (2 * E, LOOK))
    grads = add_up(swap(grads.reshape(YH * Z, 8, LOOK), ("yh", "z"))).reshape(4, E)
    return grads, logits.reshape(N)


def solution(mesh):
    fine = Mesh(mesh.devices.reshape(X, YH, CORES, Z, YL), REP + MP)
    both = REP + MP
    return jax.shard_map(
        shards,
        mesh=fine,
        in_specs=(
            P(MP, None),
            P(MP, None),
            P(REP, MP),
            P(),
            P(None, both),
            P(both),
            P(),
            P(),
            P(),
            P(),
            P(),
            P(),
            P(),
        ),
        out_specs=(P(REP, MP), P(both)),
        check_vma=False,
    )
```
